256 devices in a mesh: owner: 128 (over x, z, y), replica: 2 (over core).
Axes of the slice: x: 4, y: 4, z: 8, core: 2. Of those that a mesh axis runs over, the one named last changes fastest.
Arguments:
- queries: bfloat16 [2048, 32, 128], P(('owner', 'replica')), may hold values from -8 to 8
- pages: bfloat16 [128, 1024, 128], P('owner'), may hold values from -3 to 3
- pair_page: int32 [16384, 1], P(('owner', 'replica')), may hold values from 0 to 127, as said below
- pair_query: int32 [16384], P(('owner', 'replica')), may hold values from 0 to 7
- pair_label: int32 [16384], P(('owner', 'replica')), may hold values 0 or 1
- hot_pages: int32 [2], replicated, may hold values from 0 to 127, as said below
Outputs:
- query_grad: bfloat16 [2048, 32, 128], P(('owner', 'replica'))
- page_grad: bfloat16 [128, 1024, 128], P('owner', 'replica')
The draws below stay inside these ranges and needn't reach their ends.
Inputs may be any that keep to these rules, and one draw needn't show every extreme that they name: `pair_page`: the rows of one device name no page more than 2 times, and some page exactly 2 times. `hot_pages`: 2 different page numbers; the last page is always among them.
All inputs are finite; a program needn't handle non-finite values. No bound on the sum of `pair_label` on one device may be relied on, other than what follows from the above.
Results may differ from the reference program's by a relative error of at most 0.0085.
Values may be sent and summed in bfloat16 or wider, within the bound.
No kernel may reach another device: no remote copies, remote signals or barrier semaphores. Data moves between devices by JAX's collectives and lax.ppermute only.
A program may use at most 64 MiB of HBM per device.

```python
import math
import jax
import jax.numpy as jnp
from jax import lax

W = 128
QT = 32
PATCHES = 1024
HOT = 2
Q_DEV = 8
PAIR_DEV = 64
CAP = 2
PAGES = 128
QUERIES = 2048
PAIRS = 16384


def shared_draw(key):
    page_key = jax.random.fold_in(key, 11)
    query_key = jax.random.fold_in(key, 12)
    spread = W ** (-0.25)
    page_vals = spread * jax.random.normal(page_key, (PAGES, PATCHES, W), jnp.float32)
    query_vals = spread * jax.random.normal(query_key, (QUERIES, QT, W), jnp.float32)
    return (jnp.clip(page_vals, -3.0, 3.0), jnp.clip(query_vals, -8.0, 8.0))


def draw_pages(key, part):
    return shared_draw(key)[0].astype(jnp.bfloat16)


def draw_queries(key, part):
    return shared_draw(key)[1].astype(jnp.bfloat16)


def hot_list(key):
    others = jax.random.permutation(jax.random.fold_in(key, 21), PAGES - 1)[:HOT - 1].astype(jnp.int32)
    last_page = jnp.full((1,), PAGES - 1, jnp.int32)
    return jnp.concatenate([last_page, others]).astype(jnp.int32)


def page_lists(key):
    flagged = hot_list(key)
    numbers = jnp.arange(PAGES, dtype=jnp.int32)
    is_flagged = jnp.any(numbers[:, None] == flagged[None, :], axis=1).astype(jnp.int32)

    def one_device(device):
        device_key = jax.random.fold_in(jax.random.fold_in(key, 22), device)
        shuffled = jax.random.permutation(jax.random.fold_in(device_key, 1), PAGES).astype(jnp.int32)
        ranking = is_flagged[shuffled] * PAGES + numbers
        cold_first = shuffled[jnp.argsort(ranking, stable=True)]
        others = jnp.tile(cold_first[:PAGES - HOT], CAP)[:PAIR_DEV - HOT * CAP]
        listed = jnp.concatenate([jnp.repeat(flagged, CAP), others]).astype(jnp.int32)
        mixing = jax.random.permutation(jax.random.fold_in(device_key, 2), PAIR_DEV)
        return listed[mixing]
    rows = jax.vmap(one_device)(jnp.arange(PAIRS // PAIR_DEV, dtype=jnp.int32))
    return rows.reshape(PAIRS, 1).astype(jnp.int32)


def draw_pair_page(key, part):
    return page_lists(key)


def draw_hot_pages(key, part):
    return hot_list(key)


def with_ends(drawn, rng, least, high):
    dims = drawn.shape
    index_at = [jax.random.randint(jax.random.fold_in(rng, axis), (), 0, dims[axis]) for axis in range(len(dims))]
    drawn = drawn.at[tuple(index_at)].set(least)
    longest = dims.index(max(dims))
    index_at[longest] = (index_at[longest] + 1) % dims[longest]
    return drawn.at[tuple(index_at)].set(high)


def setup_inputs(seed: int = 0) -> dict:
    keys = jax.random.split(jax.random.key(seed), 7)
    queries = draw_queries(jax.random.fold_in(keys[6], 71), 0)
    pages = draw_pages(jax.random.fold_in(keys[6], 71), 0)
    pair_page = draw_pair_page(jax.random.fold_in(keys[6], 71), 0)
    pair_query = with_ends(jax.random.randint(keys[3], (PAIRS,), 0, Q_DEV), jax.random.fold_in(keys[3], 1), 0, Q_DEV - 1).astype(jnp.int32)
    pair_label = with_ends((jax.random.randint(keys[4], (PAIRS,), 0, 4) < 1).astype(jnp.int32), jax.random.fold_in(keys[4], 1), 0, 1)
    hot_pages = draw_hot_pages(jax.random.fold_in(keys[6], 71), 0)
    return {"queries": queries, "pages": pages, "pair_page": pair_page, "pair_query": pair_query, "pair_label": pair_label, "hot_pages": hot_pages}


SHARPNESS = 4.0
SLOPE_SCALE = 0.5
HOT_SHIFT = 2.0


def reference(queries, pages, pair_page, pair_query, pair_label, hot_pages):
    owner_ids = pair_page[:, 0].astype(jnp.int32)
    query_ids = ((jnp.arange(PAIRS, dtype=jnp.int32) // PAIR_DEV) * Q_DEV + pair_query).astype(jnp.int32)
    labels = pair_label.astype(jnp.float32)
    hot_flag = jnp.any(owner_ids[:, None] == hot_pages[None, :].astype(jnp.int32), axis=1).astype(jnp.float32)
    offset = -SLOPE_SCALE * QT * (math.log(PATCHES) / SHARPNESS + SHARPNESS / 2.0)
    group_size = 64
    groups = PAIRS // group_size

    def step(carry, inputs):
        owner_part, query_part, label_part, hot_part = inputs
        query_rows = queries[query_part].astype(jnp.float32)
        page_rows = pages[owner_part].astype(jnp.float32)
        logits = SHARPNESS * jnp.einsum("btw,bpw->btp", query_rows, page_rows)
        peak = jnp.max(logits, axis=2, keepdims=True)
        expo = jnp.exp(logits - peak)
        totals = jnp.sum(expo, axis=2, keepdims=True)
        log_total = peak + jnp.log(totals)
        score = jnp.sum(log_total[:, :, 0], axis=1) / SHARPNESS
        logit = SLOPE_SCALE * score + offset - HOT_SHIFT * hot_part
        slope = SLOPE_SCALE * (jax.nn.sigmoid(logit) - label_part)
        weight = (expo / totals * slope[:, None, None]).astype(jnp.bfloat16)
        weight_wide = weight.astype(jnp.float32)
        grads = jnp.einsum("btp,bpw->btw", weight_wide, page_rows).astype(jnp.bfloat16)
        page_part = jnp.einsum("btp,btw->bpw", weight_wide, query_rows)
        carry = carry.at[owner_part].add(page_part)
        return carry, grads

    start = jnp.zeros((PAGES, PATCHES, W), jnp.float32)
    final, parts = lax.scan(step, start, (owner_ids.reshape(groups, group_size), query_ids.reshape(groups, group_size), labels.reshape(groups, group_size), hot_flag.reshape(groups, group_size)))
    query_grad = jax.ops.segment_sum(parts.reshape(PAIRS, QT, W).astype(jnp.float32), query_ids, num_segments=QUERIES)
    return query_grad.astype(jnp.bfloat16), final.astype(jnp.bfloat16)
```

```python
import functools
import math

import jax
import jax.numpy as jnp
from jax import lax
from jax.experimental import pallas as pl
from jax.experimental.pallas import tpu as pltpu
from jax.sharding import Mesh, PartitionSpec as P

SHARPNESS = 4.0
SLOPE_SCALE = 0.5
HOT_SHIFT = 2.0

NX, NZ, NY, NC = 4, 8, 4, 2
PLANE = NX * NY
QT = 32
W = 128
Q_DEV = 8
PAIR_DEV = 64
PATCHES = 1024
HALF = PATCHES // 2
CAP = 2
ROWS = Q_DEV * QT
SEND_ROWS = ROWS + 16
ENTRIES = NZ * CAP
GROUP = 8
SLOTS = PLANE * CAP
LIST = SLOTS + GROUP


def pack_kernel(page_ref, query_ref, label_ref, rows_ref, out_ref):
    dest = lax.broadcasted_iota(jnp.int32, (PLANE, W), 0)
    lane = lax.broadcasted_iota(jnp.int32, (PLANE, W), 1)
    entry = lane % ENTRIES
    rank = entry % CAP
    wanted = (dest // NY) * (NZ * NY) + (entry // CAP) * NY + dest % NY
    is_query = lane < ENTRIES
    is_label = jnp.logical_and(lane >= ENTRIES, lane < 2 * ENTRIES)

    def visit(i, carry):
        table, seen = carry
        hit = wanted == page_ref[i]
        value = jnp.where(is_query, query_ref[i] + 1, jnp.where(is_label, label_ref[i], 0))
        table = jnp.where(jnp.logical_and(hit, seen == rank), value, table)
        return table, seen + hit.astype(jnp.int32)

    zeros = jnp.zeros((PLANE, W), jnp.int32)
    table, _ = lax.fori_loop(0, PAIR_DEV, visit, (zeros, zeros), unroll=8)
    table = table.astype(jnp.float32)
    rows = rows_ref[...]
    for d in range(PLANE):
        out_ref[d, :ROWS, :] = rows
        out_ref[d, ROWS:, :] = jnp.broadcast_to(table[d : d + 1, :], (16, W)).astype(jnp.bfloat16)


def score_kernel(
    offset, place_ref, hot_ref, table_ref, got_ref, mine_ref, other_ref,
    query_out, mine_out, other_out,
    slot_query, slot_label, tokens, expo, query_acc, mine_acc, other_acc,
):
    rows = GROUP * QT
    query_acc[...] = jnp.zeros_like(query_acc)
    first_page = place_ref[0]

    def per_page(page, _):
        page_id = first_page + page * NY
        hot = jnp.logical_or(hot_ref[0] == page_id, hot_ref[1] == page_id)
        shift = jnp.where(hot, HOT_SHIFT, 0.0).astype(jnp.float32)

        count = jnp.int32(0)
        for s in range(PLANE):
            for r in range(CAP):
                code = table_ref[s, page * CAP + r]
                slot_query[count] = s * Q_DEV + code - 1
                slot_label[count] = table_ref[s, ENTRIES + page * CAP + r]
                count = count + (code > 0).astype(jnp.int32)
        for g in range(GROUP - 1):
            slot_query[count + g] = 0
            slot_label[count + g] = 0

        mine_acc[...] = jnp.zeros_like(mine_acc)
        other_acc[...] = jnp.zeros_like(other_acc)
        mine = mine_ref.at[page]
        other = other_ref.at[page]

        def per_group(step, _):
            base = step * GROUP
            for g in range(GROUP):
                q = slot_query[base + g]
                src = q // Q_DEV
                tokens[g * QT : (g + 1) * QT, :] = got_ref[
                    src, pl.ds(pl.multiple_of((q % Q_DEV) * QT, QT), QT), :
                ]
            tok = tokens[...]
            dims = (((1,), (1,)), ((), ()))
            la = lax.dot_general(tok, mine[...], dims, preferred_element_type=jnp.float32)
            lb = lax.dot_general(tok, other[...], dims, preferred_element_type=jnp.float32)
            peak = jnp.maximum(
                jnp.max(la, axis=1, keepdims=True), jnp.max(lb, axis=1, keepdims=True)
            )
            ea = jnp.exp(SHARPNESS * (la - peak))
            eb = jnp.exp(SHARPNESS * (lb - peak))
            totals = jnp.sum(ea, axis=1, keepdims=True) + jnp.sum(eb, axis=1, keepdims=True)
            expo[:, :HALF] = ea.astype(jnp.bfloat16)
            expo[:, HALF:] = eb.astype(jnp.bfloat16)
            lse = SHARPNESS * peak + jnp.log(totals)
            scales = []
            for g in range(GROUP):
                score = jnp.sum(lse[g * QT : (g + 1) * QT], axis=0, keepdims=True) / SHARPNESS
                logit = SLOPE_SCALE * score + offset - shift
                label = slot_label[base + g].astype(jnp.float32)
                live = jnp.where(base + g < count, SLOPE_SCALE, 0.0)
                slope = live * (1.0 / (1.0 + jnp.exp(-logit)) - label)
                scales.append(slope / totals[g * QT : (g + 1) * QT])
            scale = jnp.concatenate(scales, axis=0)
            weight = expo[...]
            grads = jnp.dot(weight[:, :HALF], mine[...], preferred_element_type=jnp.float32)
            grads += jnp.dot(weight[:, HALF:], other[...], preferred_element_type=jnp.float32)
            grads = grads * scale
            scaled = (tok.astype(jnp.float32) * scale).astype(jnp.bfloat16)
            dims = (((0,), (0,)), ((), ()))
            mine_acc[...] += lax.dot_general(
                weight[:, :HALF], scaled, dims, preferred_element_type=jnp.float32
            )
            other_acc[...] += lax.dot_general(
                weight[:, HALF:], scaled, dims, preferred_element_type=jnp.float32
            )
            for g in range(GROUP):
                at = pl.ds(pl.multiple_of(slot_query[base + g] * QT, QT), QT)
                query_acc[at, :] += grads[g * QT : (g + 1) * QT]
            return 0

        lax.fori_loop(0, (count + GROUP - 1) // GROUP, per_group, 0)
        mine_out[page] = mine_acc[...].astype(jnp.bfloat16)
        other_out[page] = other_acc[...].astype(jnp.bfloat16)
        return 0

    lax.fori_loop(0, NZ, per_page, 0)
    query_out[...] = query_acc[...].astype(jnp.bfloat16)


def exchange(array, axes):
    return lax.all_to_all(array, axes, split_axis=0, concat_axis=0, tiled=True)


def swap_cores(array):
    return lax.ppermute(array, "core", [(0, 1), (1, 0)])


def shards(queries, pages, pair_page, pair_query, pair_label, hot_pages):
    offset = -SLOPE_SCALE * QT * (math.log(PATCHES) / SHARPNESS + SHARPNESS / 2.0)
    smem = pl.BlockSpec(memory_space=pltpu.SMEM)
    vmem = pl.BlockSpec(memory_space=pltpu.VMEM)
    send = pl.pallas_call(
        pack_kernel,
        out_shape=jax.ShapeDtypeStruct((PLANE, SEND_ROWS, W), jnp.bfloat16),
        in_specs=[smem, smem, smem, vmem],
        out_specs=vmem,
    )(pair_page[:, 0], pair_query, pair_label, queries.reshape(ROWS, W))
    core = lax.axis_index("core")
    half = lax.dynamic_slice(pages[0], (core * HALF, 0), (HALF, W))
    mine = exchange(jnp.broadcast_to(half[None], (NZ, HALF, W)), "z")
    other = swap_cores(mine)
    got = exchange(send, ("x", "y"))
    table = got[:, ROWS, : 2 * ENTRIES].astype(jnp.int32)
    place = (lax.axis_index("x") * (NZ * NY) + lax.axis_index("y")).reshape(1)
    query_part, mine_part, other_part = pl.pallas_call(
        functools.partial(score_kernel, offset),
        out_shape=(
            jax.ShapeDtypeStruct((PLANE * ROWS, W), jnp.bfloat16),
            jax.ShapeDtypeStruct((NZ, HALF, W), jnp.bfloat16),
            jax.ShapeDtypeStruct((NZ, HALF, W), jnp.bfloat16),
        ),
        in_specs=[smem, smem, smem, vmem, vmem, vmem],
        out_specs=(vmem, vmem, vmem),
        scratch_shapes=[
            pltpu.SMEM((LIST,), jnp.int32),
            pltpu.SMEM((LIST,), jnp.int32),
            pltpu.VMEM((GROUP * QT, W), jnp.bfloat16),
            pltpu.VMEM((GROUP * QT, PATCHES), jnp.bfloat16),
            pltpu.VMEM((PLANE * ROWS, W), jnp.float32),
            pltpu.VMEM((HALF, W), jnp.float32),
            pltpu.VMEM((HALF, W), jnp.float32),
        ],
        compiler_params=pltpu.CompilerParams(vmem_limit_bytes=48 << 20),
    )(place, hot_pages, table, got, mine, other)
    page_terms = mine_part.astype(jnp.float32) + swap_cores(other_part).astype(jnp.float32)
    page_back = exchange(page_terms.astype(jnp.bfloat16), "z")
    query_back = exchange(query_part.reshape(PLANE, ROWS, W), ("x", "y"))
    query_grad = jnp.sum(query_back.astype(jnp.float32), axis=0).astype(jnp.bfloat16)
    page_grad = jnp.sum(page_back.astype(jnp.float32), axis=0).astype(jnp.bfloat16)
    return query_grad.reshape(Q_DEV, QT, W), page_grad[None]


def solution(mesh):
    torus = Mesh(mesh.devices.reshape(NX, NZ, NY, NC), ("x", "z", "y", "core"))
    owner = ("x", "z", "y")
    device = ("x", "z", "y", "core")
    return jax.shard_map(
        shards,
        mesh=torus,
        in_specs=(P(device), P(owner), P(device), P(device), P(device), P()),
        out_specs=(P(device), P(owner, "core")),
        check_vma=False,
    )
```

```python
import functools
import math

import jax
import jax.numpy as jnp
from jax import lax
from jax.experimental import pallas as pl
from jax.experimental.pallas import tpu as pltpu
from jax.sharding import Mesh, PartitionSpec as P

SHARPNESS = 4.0
SLOPE_SCALE = 0.5
HOT_SHIFT = 2.0

NX, NZ, NY, NC = 4, 8, 4, 2
PLANE = NX * NY
QT = 32
W = 128
Q_DEV = 8
PAIR_DEV = 64
PATCHES = 1024
HALF = PATCHES // 2
CAP = 2
ROWS = Q_DEV * QT
SEND_ROWS = ROWS + 16
ENTRIES = NZ * CAP
GROUP = 8
SLOTS = PLANE * CAP
LIST = SLOTS + GROUP
STEPS = (0, -1, 1, 4, -2, 3, 2, -3)


def pack_kernel(page_ref, query_ref, label_ref, rows_ref, out_ref):
    dest = lax.broadcasted_iota(jnp.int32, (PLANE, W), 0)
    lane = lax.broadcasted_iota(jnp.int32, (PLANE, W), 1)
    entry = lane % ENTRIES
    rank = entry % CAP
    wanted = (dest // NY) * (NZ * NY) + (entry // CAP) * NY + dest % NY
    is_query = lane < ENTRIES
    is_label = jnp.logical_and(lane >= ENTRIES, lane < 2 * ENTRIES)

    def visit(i, carry):
        table, seen = carry
        hit = wanted == page_ref[i]
        value = jnp.where(is_query, query_ref[i] + 1, jnp.where(is_label, label_ref[i], 0))
        table = jnp.where(jnp.logical_and(hit, seen == rank), value, table)
        return table, seen + hit.astype(jnp.int32)

    zeros = jnp.zeros((PLANE, W), jnp.int32)
    table, _ = lax.fori_loop(0, PAIR_DEV, visit, (zeros, zeros), unroll=8)
    table = table.astype(jnp.float32)
    rows = rows_ref[...]
    for d in range(PLANE):
        out_ref[d, :ROWS, :] = rows
        out_ref[d, ROWS:, :] = jnp.broadcast_to(table[d : d + 1, :], (16, W)).astype(jnp.bfloat16)


def score_kernel(
    offset, column_ref, hot_ref, table_ref, got_ref, mine_ref, other_ref,
    query_out, mine_out, other_out,
    slot_query, slot_label, tokens, expo, query_acc, mine_acc, other_acc,
):
    rows = GROUP * QT
    query_acc[...] = jnp.zeros_like(query_acc)
    first_page = column_ref[NZ]

    def per_page(page, _):
        height = column_ref[page]
        page_id = first_page + height * NY
        hot = jnp.logical_or(hot_ref[0] == page_id, hot_ref[1] == page_id)
        shift = jnp.where(hot, HOT_SHIFT, 0.0).astype(jnp.float32)

        count = jnp.int32(0)
        for s in range(PLANE):
            for r in range(CAP):
                code = table_ref[s, height * CAP + r]
                slot_query[count] = s * Q_DEV + code - 1
                slot_label[count] = table_ref[s, ENTRIES + height * CAP + r]
                count = count + (code > 0).astype(jnp.int32)
        for g in range(GROUP - 1):
            slot_query[count + g] = 0
            slot_label[count + g] = 0

        mine_acc[...] = jnp.zeros_like(mine_acc)
        other_acc[...] = jnp.zeros_like(other_acc)
        mine = mine_ref.at[page]
        other = other_ref.at[page]

        def per_group(step, _):
            base = step * GROUP
            for g in range(GROUP):
                q = slot_query[base + g]
                src = q // Q_DEV
                tokens[g * QT : (g + 1) * QT, :] = got_ref[
                    src, pl.ds(pl.multiple_of((q % Q_DEV) * QT, QT), QT), :
                ]
            tok = tokens[...]
            dims = (((1,), (1,)), ((), ()))
            la = lax.dot_general(tok, mine[...], dims, preferred_element_type=jnp.float32)
            lb = lax.dot_general(tok, other[...], dims, preferred_element_type=jnp.float32)
            peak = jnp.maximum(
                jnp.max(la, axis=1, keepdims=True), jnp.max(lb, axis=1, keepdims=True)
            )
            ea = jnp.exp(SHARPNESS * (la - peak))
            eb = jnp.exp(SHARPNESS * (lb - peak))
            totals = jnp.sum(ea, axis=1, keepdims=True) + jnp.sum(eb, axis=1, keepdims=True)
            expo[:, :HALF] = ea.astype(jnp.bfloat16)
            expo[:, HALF:] = eb.astype(jnp.bfloat16)
            lse = SHARPNESS * peak + jnp.log(totals)
            scales = []
            for g in range(GROUP):
                score = jnp.sum(lse[g * QT : (g + 1) * QT], axis=0, keepdims=True) / SHARPNESS
                logit = SLOPE_SCALE * score + offset - shift
                label = slot_label[base + g].astype(jnp.float32)
                live = jnp.where(base + g < count, SLOPE_SCALE, 0.0)
                slope = live * (1.0 / (1.0 + jnp.exp(-logit)) - label)
                scales.append(slope / totals[g * QT : (g + 1) * QT])
            scale = jnp.concatenate(scales, axis=0)
            weight = expo[...]
            grads = jnp.dot(weight[:, :HALF], mine[...], preferred_element_type=jnp.float32)
            grads += jnp.dot(weight[:, HALF:], other[...], preferred_element_type=jnp.float32)
            grads = grads * scale
            scaled = (tok.astype(jnp.float32) * scale).astype(jnp.bfloat16)
            dims = (((0,), (0,)), ((), ()))
            mine_acc[...] += lax.dot_general(
                weight[:, :HALF], scaled, dims, preferred_element_type=jnp.float32
            )
            other_acc[...] += lax.dot_general(
                weight[:, HALF:], scaled, dims, preferred_element_type=jnp.float32
            )
            for g in range(GROUP):
                at = pl.ds(pl.multiple_of(slot_query[base + g] * QT, QT), QT)
                query_acc[at, :] += grads[g * QT : (g + 1) * QT]
            return 0

        lax.fori_loop(0, (count + GROUP - 1) // GROUP, per_group, 0)
        mine_out[page] = mine_acc[...].astype(jnp.bfloat16)
        other_out[page] = other_acc[...].astype(jnp.bfloat16)
        return 0

    lax.fori_loop(0, NZ, per_page, 0)
    query_out[...] = query_acc[...].astype(jnp.bfloat16)


def exchange(array, axes):
    return lax.all_to_all(array, axes, split_axis=0, concat_axis=0, tiled=True)


def swap_cores(array):
    return lax.ppermute(array, "core", [(0, 1), (1, 0)])


def move(array, step):
    return lax.ppermute(array, "z", [(i, (i + step) % NZ) for i in range(NZ)])


def gather_column(half):
    below, above, across = move(half, 1), move(half, -1), move(half, 4)
    far_below = move(jnp.stack([below, across]), 1)
    far_above = move(jnp.stack([above, across]), -1)
    return jnp.concatenate([jnp.stack([half, below, above, across]), far_below, far_above])


def reduce_column(terms):
    sent = terms.astype(jnp.bfloat16)
    from_below, from_above = move(sent[6:8], 1), move(sent[4:6], -1)
    up = (terms[2] + from_below[0].astype(jnp.float32)).astype(jnp.bfloat16)
    down = (terms[1] + from_above[0].astype(jnp.float32)).astype(jnp.bfloat16)
    over = terms[3] + from_below[1].astype(jnp.float32) + from_above[1].astype(jnp.float32)
    over = over.astype(jnp.bfloat16)
    total = terms[0]
    for part in (move(up, 1), move(down, -1), move(over, 4)):
        total = total + part.astype(jnp.float32)
    return total.astype(jnp.bfloat16)


def shards(queries, pages, pair_page, pair_query, pair_label, hot_pages):
    offset = -SLOPE_SCALE * QT * (math.log(PATCHES) / SHARPNESS + SHARPNESS / 2.0)
    smem = pl.BlockSpec(memory_space=pltpu.SMEM)
    vmem = pl.BlockSpec(memory_space=pltpu.VMEM)
    core = lax.axis_index("core")
    half = lax.dynamic_slice(pages[0], (core * HALF, 0), (HALF, W))
    send = pl.pallas_call(
        pack_kernel,
        out_shape=jax.ShapeDtypeStruct((PLANE, SEND_ROWS, W), jnp.bfloat16),
        in_specs=[smem, smem, smem, vmem],
        out_specs=vmem,
    )(pair_page[:, 0], pair_query, pair_label, queries.reshape(ROWS, W))
    mine = gather_column(half)
    other = swap_cores(mine)
    got = exchange(send, ("x", "y"))
    table = got[:, ROWS, : 2 * ENTRIES].astype(jnp.int32)
    heights = (lax.axis_index("z") + jnp.array(STEPS, jnp.int32)) % NZ
    first_page = lax.axis_index("x") * (NZ * NY) + lax.axis_index("y")
    column = jnp.concatenate([heights, first_page.reshape(1)])
    query_part, mine_part, other_part = pl.pallas_call(
        functools.partial(score_kernel, offset),
        out_shape=(
            jax.ShapeDtypeStruct((PLANE * ROWS, W), jnp.bfloat16),
            jax.ShapeDtypeStruct((NZ, HALF, W), jnp.bfloat16),
            jax.ShapeDtypeStruct((NZ, HALF, W), jnp.bfloat16),
        ),
        in_specs=[smem, smem, smem, vmem, vmem, vmem],
        out_specs=(vmem, vmem, vmem),
        scratch_shapes=[
            pltpu.SMEM((LIST,), jnp.int32),
            pltpu.SMEM((LIST,), jnp.int32),
            pltpu.VMEM((GROUP * QT, W), jnp.bfloat16),
            pltpu.VMEM((GROUP * QT, PATCHES), jnp.bfloat16),
            pltpu.VMEM((PLANE * ROWS, W), jnp.float32),
            pltpu.VMEM((HALF, W), jnp.float32),
            pltpu.VMEM((HALF, W), jnp.float32),
        ],
        compiler_params=pltpu.CompilerParams(vmem_limit_bytes=48 << 20),
    )(column, hot_pages, table, got, mine, other)
    terms = mine_part.astype(jnp.float32) + swap_cores(other_part).astype(jnp.float32)
    query_back = exchange(query_part.reshape(PLANE, ROWS, W), ("x", "y"))
    page_grad = reduce_column(terms)
    query_grad = jnp.sum(query_back.astype(jnp.float32), axis=0).astype(jnp.bfloat16)
    return query_grad.reshape(Q_DEV, QT, W), page_grad[None]


def solution(mesh):
    torus = Mesh(mesh.devices.reshape(NX, NZ, NY, NC), ("x", "z", "y", "core"))
    owner = ("x", "z", "y")
    device = ("x", "z", "y", "core")
    return jax.shard_map(
        shards,
        mesh=torus,
        in_specs=(P(device), P(owner), P(device), P(device), P(device), P()),
        out_specs=(P(device), P(owner, "core")),
        check_vma=False,
    )
```

```python
import functools
import math

import jax
import jax.numpy as jnp
from jax import lax
from jax.experimental import pallas as pl
from jax.experimental.pallas import tpu as pltpu
from jax.sharding import Mesh, PartitionSpec as P

SHARPNESS = 4.0
SLOPE_SCALE = 0.5
HOT_SHIFT = 2.0

NX, NZ, NY, NC = 4, 8, 4, 2
PLANE = NX * NY
QT = 32
W = 128
Q_DEV = 8
PAIR_DEV = 64
PATCHES = 1024
HALF = PATCHES // 2
CAP = 2
ROWS = Q_DEV * QT
SEND_ROWS = ROWS + 16
ENTRIES = NZ * CAP
GROUP = 8
BLOCK = 128
ITEMS = 3
SLOTS = PLANE * CAP
LIST = SLOTS + GROUP
PART = NZ // 2
STEPS = (0, -1, 1, 4, -2, 3, 2, -3)


def pack_kernel(page_ref, query_ref, label_ref, rows_ref, out_ref):
    dest = lax.broadcasted_iota(jnp.int32, (PLANE, W), 0)
    lane = lax.broadcasted_iota(jnp.int32, (PLANE, W), 1)
    entry = lane % ENTRIES
    rank = entry % CAP
    wanted = (dest // NY) * (NZ * NY) + (entry // CAP) * NY + dest % NY
    is_query = lane < ENTRIES
    is_label = jnp.logical_and(lane >= ENTRIES, lane < 2 * ENTRIES)

    def visit(i, carry):
        table, seen = carry
        hit = wanted == page_ref[i]
        value = jnp.where(is_query, query_ref[i] + 1, jnp.where(is_label, label_ref[i], 0))
        table = jnp.where(jnp.logical_and(hit, seen == rank), value, table)
        return table, seen + hit.astype(jnp.int32)

    zeros = jnp.zeros((PLANE, W), jnp.int32)
    table, _ = lax.fori_loop(0, PAIR_DEV, visit, (zeros, zeros), unroll=8)
    table = table.astype(jnp.float32)
    rows = rows_ref[...]
    for d in range(PLANE):
        out_ref[d, :ROWS, :] = rows
        out_ref[d, ROWS:, :] = jnp.broadcast_to(table[d : d + 1, :], (16, W)).astype(jnp.bfloat16)


def score_kernel(
    offset, column_ref, hot_ref, table_ref, got_ref, mine_ref, other_ref, carried_ref,
    query_out, mine_out, other_out,
    slot_query, slot_label, item_page, item_base, item_left, turned, query_acc, page_acc, *work,
):
    rows = GROUP * QT
    if query_acc is None:
        query_acc = query_out
    token_refs, logit_refs, expo_refs = work[:ITEMS], work[ITEMS : 2 * ITEMS], work[2 * ITEMS :]
    if carried_ref is None:
        query_acc[...] = jnp.zeros_like(query_acc)
    else:
        query_acc[...] = carried_ref[...]
    page_acc[...] = jnp.zeros_like(page_acc)
    first_page = column_ref[PART]

    def list_page(page, items):
        height = column_ref[page]
        turned[page, :, :HALF] = mine_ref[page].T
        turned[page, :, HALF:] = other_ref[page].T
        start = page * LIST
        count = jnp.int32(0)
        for s in range(PLANE):
            for r in range(CAP):
                code = table_ref[s, height * CAP + r]
                slot_query[start + count] = s * Q_DEV + code - 1
                slot_label[start + count] = table_ref[s, ENTRIES + height * CAP + r]
                count = count + (code > 0).astype(jnp.int32)
        for g in range(GROUP - 1):
            slot_query[start + count + g] = 0
            slot_label[start + count + g] = 0
        for j in range(SLOTS // GROUP):
            item_page[items] = page
            item_base[items] = start + j * GROUP
            item_left[items] = count - j * GROUP
            items = items + (count > j * GROUP).astype(jnp.int32)
        return items

    items = lax.fori_loop(0, PART, list_page, jnp.int32(0))
    for g in range(GROUP):
        slot_query[PART * LIST + g] = 0
        slot_label[PART * LIST + g] = 0
    for u in range(ITEMS):
        item_page[items + u] = 0
        item_base[items + u] = PART * LIST
        item_left[items + u] = 0

    def per_round(step, _):
        at = [step * ITEMS + u for u in range(ITEMS)]
        page = [item_page[i] for i in at]
        base = [item_base[i] for i in at]
        left = [item_left[i] for i in at]
        query = [[slot_query[b + g] for g in range(GROUP)] for b in base]
        for u in range(ITEMS):
            for g in range(GROUP):
                token_refs[u][g * QT : (g + 1) * QT, :] = got_ref[
                    lax.shift_right_logical(query[u][g], 3),
                    pl.ds(pl.multiple_of(lax.bitwise_and(query[u][g], Q_DEV - 1) * QT, QT), QT),
                    :,
                ]
        dims = (((1,), (1,)), ((), ()))
        peaks, lses, inverses = [], [], []
        for u in range(ITEMS):
            tok = token_refs[u][...]
            peak = None
            for c in range(PATCHES // BLOCK):
                part = (mine_ref, other_ref)[c * BLOCK // HALF]
                first = c * BLOCK % HALF
                block = lax.dot_general(
                    part[page[u], first : first + BLOCK, :], tok, dims,
                    preferred_element_type=jnp.float32,
                )
                logit_refs[u][c * BLOCK : (c + 1) * BLOCK, :] = block
                top = jnp.max(block.reshape(BLOCK // 8, 8, rows), axis=0)
                peak = top if peak is None else jnp.maximum(peak, top)
            peaks.append(jnp.max(peak, axis=0, keepdims=True))
        for u in range(ITEMS):
            total = None
            for c in range(PATCHES // BLOCK):
                piece = logit_refs[u][c * BLOCK : (c + 1) * BLOCK, :]
                e = jnp.exp(SHARPNESS * (piece - peaks[u]))
                expo_refs[u][c * BLOCK : (c + 1) * BLOCK, :] = e.astype(jnp.bfloat16)
                low = jnp.sum(e.reshape(BLOCK // 8, 8, rows), axis=0)
                total = low if total is None else total + low
            total = jnp.sum(total, axis=0, keepdims=True)
            lse = SHARPNESS * peaks[u] + jnp.log(total)
            lses.append(jnp.broadcast_to(lse, (W, rows)).T)
            inverses.append(jnp.broadcast_to(1.0 / total, (W, rows)).T)
        grads = [
            jnp.dot(turned[page[u]], expo_refs[u][...], preferred_element_type=jnp.float32).T
            for u in range(ITEMS)
        ]
        scale = []
        for u in range(ITEMS):
            page_id = first_page + column_ref[page[u]] * NY
            hot = jnp.logical_or(hot_ref[0] == page_id, hot_ref[1] == page_id)
            shift = jnp.where(hot, HOT_SHIFT, 0.0).astype(jnp.float32)
            parts = []
            for g in range(GROUP):
                mine = slice(g * QT, (g + 1) * QT)
                score = jnp.sum(lses[u][mine], axis=0, keepdims=True) / SHARPNESS
                logit = SLOPE_SCALE * score + offset - shift
                label = slot_label[base[u] + g].astype(jnp.float32)
                live = jnp.where(g < left[u], SLOPE_SCALE, 0.0)
                slope = live * (1.0 / (1.0 + jnp.exp(-logit)) - label)
                parts.append(slope * inverses[u][mine])
            scale.append(jnp.concatenate(parts, axis=0))
        for u in range(ITEMS):
            scaled = (token_refs[u][...].astype(jnp.float32) * scale[u]).astype(jnp.bfloat16)
            page_acc[page[u]] += jnp.dot(
                expo_refs[u][...], scaled, preferred_element_type=jnp.float32
            )
        for u in range(ITEMS):
            grad = grads[u] * scale[u]
            for g in range(GROUP):
                rows_at = pl.ds(pl.multiple_of(query[u][g] * QT, QT), QT)
                query_acc[rows_at, :] += grad[g * QT : (g + 1) * QT]
        return 0

    lax.fori_loop(0, (items + ITEMS - 1) // ITEMS, per_round, 0)
    for k in range(PART):
        mine_out[k] = page_acc[k, :HALF, :].astype(jnp.bfloat16)
        other_out[k] = page_acc[k, HALF:, :].astype(jnp.bfloat16)
    if query_out is not query_acc:
        query_out[...] = query_acc[...].astype(jnp.bfloat16)


def exchange(array, axes):
    return lax.all_to_all(array, axes, split_axis=0, concat_axis=0, tiled=True)


def swap_cores(array):
    return lax.ppermute(array, "core", [(0, 1), (1, 0)])


def move(array, step):
    return lax.ppermute(array, "z", [(i, (i + step) % NZ) for i in range(NZ)])


def gather_column(half):
    below, above, across = move(half, 1), move(half, -1), move(half, 4)
    far_below = move(jnp.stack([below, across]), 1)
    far_above = move(jnp.stack([above, across]), -1)
    return jnp.stack([half, below, above, across]), jnp.concatenate([far_below, far_above])


def reduce_column(near, from_below, from_above):
    up = (near[2] + from_below[0].astype(jnp.float32)).astype(jnp.bfloat16)
    down = (near[1] + from_above[0].astype(jnp.float32)).astype(jnp.bfloat16)
    over = near[3] + from_below[1].astype(jnp.float32) + from_above[1].astype(jnp.float32)
    over = over.astype(jnp.bfloat16)
    total = near[0]
    for part in (move(up, 1), move(down, -1), move(over, 4)):
        total = total + part.astype(jnp.float32)
    return total.astype(jnp.bfloat16)


def first_kernel(offset, *refs):
    score_kernel(offset, *refs[:6], None, *refs[6:15], None, *refs[15:])


def second_kernel(offset, *refs):
    score_kernel(offset, *refs)


def score(column, hot_pages, table, got, mine, other, carried=None):
    offset = -SLOPE_SCALE * QT * (math.log(PATCHES) / SHARPNESS + SHARPNESS / 2.0)
    smem = pl.BlockSpec(memory_space=pltpu.SMEM)
    vmem = pl.BlockSpec(memory_space=pltpu.VMEM)
    last = carried is not None
    pages = jax.ShapeDtypeStruct((PART, HALF, W), jnp.bfloat16)
    sums = jax.ShapeDtypeStruct((PLANE * ROWS, W), jnp.bfloat16 if last else jnp.float32)
    items = PART * SLOTS // GROUP + ITEMS
    rows = GROUP * QT
    scratch = [
        pltpu.SMEM((PART * LIST + GROUP,), jnp.int32),
        pltpu.SMEM((PART * LIST + GROUP,), jnp.int32),
        pltpu.SMEM((items,), jnp.int32),
        pltpu.SMEM((items,), jnp.int32),
        pltpu.SMEM((items,), jnp.int32),
        pltpu.VMEM((PART, W, PATCHES), jnp.bfloat16),
    ]
    scratch += [pltpu.VMEM((PLANE * ROWS, W), jnp.float32)] * last
    scratch += [pltpu.VMEM((PART, PATCHES, W), jnp.float32)]
    scratch += [pltpu.VMEM((rows, W), jnp.bfloat16)] * ITEMS
    scratch += [pltpu.VMEM((PATCHES, rows), jnp.float32)] * ITEMS
    scratch += [pltpu.VMEM((PATCHES, rows), jnp.bfloat16)] * ITEMS
    return pl.pallas_call(
        functools.partial(second_kernel if last else first_kernel, offset),
        out_shape=(sums, pages, pages),
        in_specs=[smem] * 3 + [vmem] * (3 + last),
        out_specs=(vmem, vmem, vmem),
        scratch_shapes=scratch,
        compiler_params=pltpu.CompilerParams(vmem_limit_bytes=40 << 20),
        cost_estimate=pl.CostEstimate(
            flops=6 * PLANE * CAP * 2 * QT * PATCHES * W * 2,
            bytes_accessed=8 << 20,
            transcendentals=PLANE * CAP * 2 * QT * PATCHES,
        ),
    )(column, hot_pages, table, got, mine, other, *([carried] if last else []))


def shards(queries, pages, pair_page, pair_query, pair_label, hot_pages):
    smem = pl.BlockSpec(memory_space=pltpu.SMEM)
    vmem = pl.BlockSpec(memory_space=pltpu.VMEM)
    core = lax.axis_index("core")
    half = lax.dynamic_slice(pages[0], (core * HALF, 0), (HALF, W))
    send = pl.pallas_call(
        pack_kernel,
        out_shape=jax.ShapeDtypeStruct((PLANE, SEND_ROWS, W), jnp.bfloat16),
        in_specs=[smem, smem, smem, vmem],
        out_specs=vmem,
    )(pair_page[:, 0], pair_query, pair_label, queries.reshape(ROWS, W))
    near, far = gather_column(half)
    other_near, other_far = swap_cores(near), swap_cores(far)
    got = exchange(send, ("x", "y"))
    table = got[:, ROWS, : 2 * ENTRIES].astype(jnp.int32)
    heights = (lax.axis_index("z") + jnp.array(STEPS, jnp.int32)) % NZ
    first_page = (lax.axis_index("x") * (NZ * NY) + lax.axis_index("y")).reshape(1)
    near_column = jnp.concatenate([heights[:PART], first_page])
    far_column = jnp.concatenate([heights[PART:], first_page])
    sums, mine_terms, other_terms = score(far_column, hot_pages, table, got, far, other_far)
    far_terms = mine_terms.astype(jnp.float32) + swap_cores(other_terms).astype(jnp.float32)
    far_terms = far_terms.astype(jnp.bfloat16)
    query_part, mine_terms, other_terms = score(
        near_column, hot_pages, table, got, near, other_near, sums
    )
    near_terms = mine_terms.astype(jnp.float32) + swap_cores(other_terms).astype(jnp.float32)
    from_below, from_above = move(far_terms[2:4], 1), move(far_terms[0:2], -1)
    query_back = exchange(query_part.reshape(PLANE, ROWS, W), ("x", "y"))
    page_grad = reduce_column(near_terms, from_below, from_above)
    query_grad = jnp.sum(query_back.astype(jnp.float32), axis=0).astype(jnp.bfloat16)
    return query_grad.reshape(Q_DEV, QT, W), page_grad[None]


def solution(mesh):
    torus = Mesh(mesh.devices.reshape(NX, NZ, NY, NC), ("x", "z", "y", "core"))
    owner = ("x", "z", "y")
    device = ("x", "z", "y", "core")
    return jax.shard_map(
        shards,
        mesh=torus,
        in_specs=(P(device), P(owner), P(device), P(device), P(device), P()),
        out_specs=(P(device), P(owner, "core")),
        check_vma=False,
    )
```

```python
import functools
import math

import jax
import jax.numpy as jnp
from jax import lax
from jax.experimental import pallas as pl
from jax.experimental.pallas import tpu as pltpu
from jax.sharding import Mesh, PartitionSpec as P

SHARPNESS = 4.0
SLOPE_SCALE = 0.5
HOT_SHIFT = 2.0

NX, NZ, NY, NC = 4, 8, 4, 2
PLANE = NX * NY
QT = 32
W = 128
Q_DEV = 8
PAIR_DEV = 64
PATCHES = 1024
HALF = PATCHES // 2
CAP = 2
ROWS = Q_DEV * QT
SEND_ROWS = ROWS + 16
ENTRIES = NZ * CAP
GROUP = 8
BLOCK = 128
LOG2 = 4.0 * math.log2(math.e)
ITEMS = 4
SLOTS = PLANE * CAP
LIST = SLOTS + GROUP
PART = NZ // 2
STEPS = (0, -1, 1, 4, -2, 3, 2, -3)


def pack_kernel(page_ref, query_ref, label_ref, core_ref, rows_ref, whole_ref, out_ref, half_ref):
    half_ref[...] = whole_ref[pl.ds(pl.multiple_of(core_ref[0] * HALF, HALF), HALF), :]
    dest = lax.broadcasted_iota(jnp.int32, (PLANE, W), 0)
    lane = lax.broadcasted_iota(jnp.int32, (PLANE, W), 1)
    entry = lane % ENTRIES
    rank = entry % CAP
    wanted = (dest // NY) * (NZ * NY) + (entry // CAP) * NY + dest % NY
    is_query = lane < ENTRIES
    is_label = jnp.logical_and(lane >= ENTRIES, lane < 2 * ENTRIES)

    def visit(i, carry):
        table, seen = carry
        hit = wanted == page_ref[i]
        value = jnp.where(is_query, query_ref[i] + 1, jnp.where(is_label, label_ref[i], 0))
        table = jnp.where(jnp.logical_and(hit, seen == rank), value, table)
        return table, seen + hit.astype(jnp.int32)

    zeros = jnp.zeros((PLANE, W), jnp.int32)
    table, _ = lax.fori_loop(0, PAIR_DEV, visit, (zeros, zeros), unroll=8)
    table = table.astype(jnp.float32)
    rows = rows_ref[...]
    for d in range(PLANE):
        out_ref[d, :ROWS, :] = rows
        out_ref[d, ROWS:, :] = jnp.broadcast_to(table[d : d + 1, :], (16, W)).astype(jnp.bfloat16)


def score_kernel(
    offset, column_ref, hot_ref, table_ref, got_ref, mine_ref, other_ref,
    query_out, far_mine, far_other, near_mine, near_other,
    slot_query, slot_label, item_page, item_base, item_left, turned, query_acc, page_acc, *work,
):
    rows = GROUP * QT
    token_refs, logit_refs, expo_refs = work[:ITEMS], work[ITEMS : 2 * ITEMS], work[2 * ITEMS :]
    query_acc[...] = jnp.zeros_like(query_acc)
    page_acc[...] = jnp.zeros_like(page_acc)
    first_page = column_ref[NZ]

    def list_page(page, items):
        height = column_ref[page]
        turned[page, :, :HALF] = mine_ref[page].T
        turned[page, :, HALF:] = other_ref[page].T
        start = page * LIST
        count = jnp.int32(0)
        for s in range(PLANE):
            for r in range(CAP):
                code = table_ref[s, height * CAP + r]
                slot_query[start + count] = s * Q_DEV + code - 1
                slot_label[start + count] = table_ref[s, ENTRIES + height * CAP + r]
                count = count + (code > 0).astype(jnp.int32)
        for g in range(GROUP - 1):
            slot_query[start + count + g] = 0
            slot_label[start + count + g] = 0
        for j in range(SLOTS // GROUP):
            item_page[items] = page
            item_base[items] = start + j * GROUP
            item_left[items] = count - j * GROUP
            items = items + (count > j * GROUP).astype(jnp.int32)
        return items

    items = lax.fori_loop(0, NZ, list_page, jnp.int32(0))
    for g in range(GROUP):
        slot_query[NZ * LIST + g] = 0
        slot_label[NZ * LIST + g] = 0
    for u in range(ITEMS):
        item_page[items + u] = 0
        item_base[items + u] = NZ * LIST
        item_left[items + u] = 0

    def per_round(step, _):
        at = [step * ITEMS + u for u in range(ITEMS)]
        page = [item_page[i] for i in at]
        base = [item_base[i] for i in at]
        left = [item_left[i] for i in at]
        query = [[slot_query[b + g] for g in range(GROUP)] for b in base]
        for u in range(ITEMS):
            for g in range(GROUP):
                token_refs[u][g * QT : (g + 1) * QT, :] = got_ref[
                    lax.shift_right_logical(query[u][g], 3),
                    pl.ds(pl.multiple_of(lax.bitwise_and(query[u][g], Q_DEV - 1) * QT, QT), QT),
                    :,
                ]
        dims = (((1,), (1,)), ((), ()))
        peaks, lses, inverses = [], [], []
        blocks = PATCHES // BLOCK
        tops, totals = [None] * ITEMS, [None] * ITEMS

        def multiply(u, c):
            part = (mine_ref, other_ref)[c * BLOCK // HALF]
            first = c * BLOCK % HALF
            block = lax.dot_general(
                part[page[u], first : first + BLOCK, :], token_refs[u][...], dims,
                preferred_element_type=jnp.float32,
            )
            logit_refs[u][c * BLOCK : (c + 1) * BLOCK, :] = block
            top = jnp.max(block.reshape(BLOCK // 8, 8, rows), axis=0)
            tops[u] = top if c == 0 else jnp.maximum(tops[u], top)

        def raise_e(u, c):
            piece = logit_refs[u][c * BLOCK : (c + 1) * BLOCK, :]
            e = jnp.exp2(LOG2 * (piece - peaks[u]))
            expo_refs[u][c * BLOCK : (c + 1) * BLOCK, :] = e.astype(jnp.bfloat16)
            low = jnp.sum(e.reshape(BLOCK // 8, 8, rows), axis=0)
            totals[u] = low if c == 0 else totals[u] + low

        grads = []
        for c in range(blocks):
            multiply(0, c)
        for u in range(ITEMS):
            peaks.append(jnp.max(tops[u], axis=0, keepdims=True))
            for c in range(blocks):
                if u + 1 < ITEMS:
                    multiply(u + 1, c)
                raise_e(u, c)
            total = jnp.sum(totals[u], axis=0, keepdims=True)
            lse = SHARPNESS * peaks[u] + jnp.log(total)
            lses.append(jnp.broadcast_to(lse, (W, rows)).T)
            inverses.append(jnp.broadcast_to(1.0 / total, (W, rows)).T)
            grads.append(
                jnp.dot(turned[page[u]], expo_refs[u][...], preferred_element_type=jnp.float32).T
            )
        scale = []
        for u in range(ITEMS):
            page_id = first_page + column_ref[page[u]] * NY
            hot = jnp.logical_or(hot_ref[0] == page_id, hot_ref[1] == page_id)
            shift = jnp.where(hot, HOT_SHIFT, 0.0).astype(jnp.float32)
            parts = []
            for g in range(GROUP):
                mine = slice(g * QT, (g + 1) * QT)
                score = jnp.sum(lses[u][mine], axis=0, keepdims=True) / SHARPNESS
                logit = SLOPE_SCALE * score + offset - shift
                label = slot_label[base[u] + g].astype(jnp.float32)
                live = jnp.where(g < left[u], SLOPE_SCALE, 0.0)
                slope = live * (1.0 / (1.0 + jnp.exp(-logit)) - label)
                parts.append(slope * inverses[u][mine])
            scale.append(jnp.concatenate(parts, axis=0))
        for u in range(ITEMS):
            scaled = (token_refs[u][...].astype(jnp.float32) * scale[u]).astype(jnp.bfloat16)
            page_acc[page[u]] += jnp.dot(
                expo_refs[u][...], scaled, preferred_element_type=jnp.float32
            )
        for u in range(ITEMS):
            grad = grads[u] * scale[u]
            for g in range(GROUP):
                rows_at = pl.ds(pl.multiple_of(query[u][g] * QT, QT), QT)
                query_acc[rows_at, :] += grad[g * QT : (g + 1) * QT]
        return 0

    lax.fori_loop(0, (items + ITEMS - 1) // ITEMS, per_round, 0)
    for k in range(PART):
        near_mine[k] = page_acc[k, :HALF, :].astype(jnp.bfloat16)
        near_other[k] = page_acc[k, HALF:, :].astype(jnp.bfloat16)
        far_mine[k] = page_acc[PART + k, :HALF, :].astype(jnp.bfloat16)
        far_other[k] = page_acc[PART + k, HALF:, :].astype(jnp.bfloat16)
    query_out[...] = query_acc[...].astype(jnp.bfloat16)


def exchange(array, axes):
    return lax.all_to_all(array, axes, split_axis=0, concat_axis=0, tiled=True)


def swap_cores(array):
    return lax.ppermute(array, "core", [(0, 1), (1, 0)])


def move(array, step):
    return lax.ppermute(array, "z", [(i, (i + step) % NZ) for i in range(NZ)])


def gather_column(half):
    below, above, across = move(half, 1), move(half, -1), move(half, 4)
    far_below = move(jnp.stack([below, across]), 1)
    far_above = move(jnp.stack([above, across]), -1)
    return jnp.concatenate([jnp.stack([half, below, above, across]), far_below, far_above])


def add(mine, other):
    return mine.astype(jnp.float32) + other.astype(jnp.float32)


def reduce_column(mine, other, from_below, from_above):
    up = (add(mine[2], other[2]) + from_below[0].astype(jnp.float32)).astype(jnp.bfloat16)
    down = (add(mine[1], other[1]) + from_above[0].astype(jnp.float32)).astype(jnp.bfloat16)
    over = (add(mine[3], other[3]) + add(from_below[1], from_above[1])).astype(jnp.bfloat16)
    total = add(mine[0], other[0])
    for part in (move(up, 1), move(down, -1), move(over, 4)):
        total = total + part.astype(jnp.float32)
    return total.astype(jnp.bfloat16)


def score(column, hot_pages, table, got, mine, other):
    offset = -SLOPE_SCALE * QT * (math.log(PATCHES) / SHARPNESS + SHARPNESS / 2.0)
    smem = pl.BlockSpec(memory_space=pltpu.SMEM)
    vmem = pl.BlockSpec(memory_space=pltpu.VMEM)
    return pl.pallas_call(
        functools.partial(score_kernel, offset),
        out_shape=(jax.ShapeDtypeStruct((PLANE * ROWS, W), jnp.bfloat16),)
        + (jax.ShapeDtypeStruct((PART, HALF, W), jnp.bfloat16),) * 4,
        in_specs=[smem, smem, smem, vmem, vmem, vmem],
        out_specs=(vmem,) * 5,
        scratch_shapes=[
            pltpu.SMEM((NZ * LIST + GROUP,), jnp.int32),
            pltpu.SMEM((NZ * LIST + GROUP,), jnp.int32),
            pltpu.SMEM((NZ * SLOTS // GROUP + ITEMS,), jnp.int32),
            pltpu.SMEM((NZ * SLOTS // GROUP + ITEMS,), jnp.int32),
            pltpu.SMEM((NZ * SLOTS // GROUP + ITEMS,), jnp.int32),
            pltpu.VMEM((NZ, W, PATCHES), jnp.bfloat16),
            pltpu.VMEM((PLANE * ROWS, W), jnp.float32),
            pltpu.VMEM((NZ, PATCHES, W), jnp.float32),
        ]
        + [pltpu.VMEM((GROUP * QT, W), jnp.bfloat16)] * ITEMS
        + [pltpu.VMEM((PATCHES, GROUP * QT), jnp.float32)] * ITEMS
        + [pltpu.VMEM((PATCHES, GROUP * QT), jnp.bfloat16)] * ITEMS,
        compiler_params=pltpu.CompilerParams(vmem_limit_bytes=26 << 20),
    )(column, hot_pages, table, got, mine, other)


def shards(queries, pages, pair_page, pair_query, pair_label, hot_pages):
    smem = pl.BlockSpec(memory_space=pltpu.SMEM)
    vmem = pl.BlockSpec(memory_space=pltpu.VMEM)
    core = lax.axis_index("core").reshape(1)
    send, half = pl.pallas_call(
        pack_kernel,
        out_shape=(
            jax.ShapeDtypeStruct((PLANE, SEND_ROWS, W), jnp.bfloat16),
            jax.ShapeDtypeStruct((HALF, W), jnp.bfloat16),
        ),
        in_specs=[smem] * 4 + [vmem] * 2,
        out_specs=(vmem, vmem),
    )(pair_page[:, 0], pair_query, pair_label, core, queries.reshape(ROWS, W), pages[0])
    mine = gather_column(half)
    other = swap_cores(mine)
    got = exchange(send, ("x", "y"))
    table = got[:, ROWS, : 2 * ENTRIES].astype(jnp.int32)
    heights = (lax.axis_index("z") + jnp.array(STEPS, jnp.int32)) % NZ
    first_page = lax.axis_index("x") * (NZ * NY) + lax.axis_index("y")
    column = jnp.concatenate([heights, first_page.reshape(1)])
    query_part, far_mine, far_other, near_mine, near_other = score(
        column, hot_pages, table, got, mine, other
    )
    far_other, near_other = swap_cores(far_other), swap_cores(near_other)
    to_above = add(far_mine[2:4], far_other[2:4]).astype(jnp.bfloat16)
    to_below = add(far_mine[0:2], far_other[0:2]).astype(jnp.bfloat16)
    from_below, from_above = move(to_above, 1), move(to_below, -1)
    query_back = exchange(query_part.reshape(PLANE, ROWS, W), ("x", "y"))
    page_grad = reduce_column(near_mine, near_other, from_below, from_above)
    query_grad = jnp.sum(query_back.astype(jnp.float32), axis=0).astype(jnp.bfloat16)
    return query_grad.reshape(Q_DEV, QT, W), page_grad[None]


def solution(mesh):
    torus = Mesh(mesh.devices.reshape(NX, NZ, NY, NC), ("x", "z", "y", "core"))
    owner = ("x", "z", "y")
    device = ("x", "z", "y", "core")
    return jax.shard_map(
        shards,
        mesh=torus,
        in_specs=(P(device), P(owner), P(device), P(device), P(device), P()),
        out_specs=(P(device), P(owner, "core")),
        check_vma=False,
    )
```

```python
import functools
import math

import jax
import jax.numpy as jnp
from jax import lax
from jax.experimental import pallas as pl
from jax.experimental.pallas import tpu as pltpu
from jax.sharding import Mesh, PartitionSpec as P

SHARPNESS = 4.0
SLOPE_SCALE = 0.5
HOT_SHIFT = 2.0

NX, NZ, NY, NC = 4, 8, 4, 2
PLANE = NX * NY
QT = 32
W = 128
Q_DEV = 8
PAIR_DEV = 64
PATCHES = 1024
HALF = PATCHES // 2
CAP = 2
ROWS = Q_DEV * QT
SEND_ROWS = ROWS + 16
ENTRIES = NZ * CAP
GROUP = 8
BLOCK = 128
LOG2 = 4.0 * math.log2(math.e)
ITEMS = 2
SLOTS = PLANE * CAP
LIST = SLOTS + GROUP
PART = NZ // 2
STEPS = (0, -1, 1, 4, -2, 3, 2, -3)


def pack_kernel(page_ref, query_ref, label_ref, core_ref, rows_ref, whole_ref, out_ref, half_ref):
    half_ref[...] = whole_ref[pl.ds(pl.multiple_of(core_ref[0] * HALF, HALF), HALF), :]
    dest = lax.broadcasted_iota(jnp.int32, (PLANE, W), 0)
    lane = lax.broadcasted_iota(jnp.int32, (PLANE, W), 1)
    entry = lane % ENTRIES
    rank = entry % CAP
    wanted = (dest // NY) * (NZ * NY) + (entry // CAP) * NY + dest % NY
    is_query = lane < ENTRIES
    is_label = jnp.logical_and(lane >= ENTRIES, lane < 2 * ENTRIES)

    def visit(i, carry):
        table, seen = carry
        hit = wanted == page_ref[i]
        value = jnp.where(is_query, query_ref[i] + 1, jnp.where(is_label, label_ref[i], 0))
        table = jnp.where(jnp.logical_and(hit, seen == rank), value, table)
        return table, seen + hit.astype(jnp.int32)

    zeros = jnp.zeros((PLANE, W), jnp.int32)
    table, _ = lax.fori_loop(0, PAIR_DEV, visit, (zeros, zeros), unroll=8)
    table = table.astype(jnp.float32)
    rows = rows_ref[...]
    for d in range(PLANE):
        out_ref[d, :ROWS, :] = rows
        out_ref[d, ROWS:, :] = jnp.broadcast_to(table[d : d + 1, :], (16, W)).astype(jnp.bfloat16)


def score_kernel(
    offset, column_ref, hot_ref, table_ref, got_ref, mine_ref, other_ref, carried_ref,
    query_out, mine_out, other_out,
    slot_query, slot_label, item_page, item_base, item_left, turned, query_acc, page_acc, *work,
):
    rows = GROUP * QT
    if query_acc is None:
        query_acc = query_out
    token_refs, logit_refs, expo_refs = work[:ITEMS], work[ITEMS : 2 * ITEMS], work[2 * ITEMS :]
    if carried_ref is None:
        query_acc[...] = jnp.zeros_like(query_acc)
    else:
        query_acc[...] = carried_ref[...]
    page_acc[...] = jnp.zeros_like(page_acc)
    first_page = column_ref[PART]

    def list_page(page, items):
        height = column_ref[page]
        turned[page, :, :HALF] = mine_ref[page].T
        turned[page, :, HALF:] = other_ref[page].T
        start = page * LIST
        count = jnp.int32(0)
        for s in range(PLANE):
            for r in range(CAP):
                code = table_ref[s, height * CAP + r]
                slot_query[start + count] = s * Q_DEV + code - 1
                slot_label[start + count] = table_ref[s, ENTRIES + height * CAP + r]
                count = count + (code > 0).astype(jnp.int32)
        for g in range(GROUP - 1):
            slot_query[start + count + g] = 0
            slot_label[start + count + g] = 0
        for j in range(SLOTS // GROUP):
            item_page[items] = page
            item_base[items] = start + j * GROUP
            item_left[items] = count - j * GROUP
            items = items + (count > j * GROUP).astype(jnp.int32)
        return items

    items = lax.fori_loop(0, PART, list_page, jnp.int32(0))
    for g in range(GROUP):
        slot_query[PART * LIST + g] = 0
        slot_label[PART * LIST + g] = 0
    for u in range(ITEMS):
        item_page[items + u] = 0
        item_base[items + u] = PART * LIST
        item_left[items + u] = 0

    def per_round(step, _):
        at = [step * ITEMS + u for u in range(ITEMS)]
        page = [item_page[i] for i in at]
        base = [item_base[i] for i in at]
        left = [item_left[i] for i in at]
        query = [[slot_query[b + g] for g in range(GROUP)] for b in base]
        for u in range(ITEMS):
            for g in range(GROUP):
                token_refs[u][g * QT : (g + 1) * QT, :] = got_ref[
                    lax.shift_right_logical(query[u][g], 3),
                    pl.ds(pl.multiple_of(lax.bitwise_and(query[u][g], Q_DEV - 1) * QT, QT), QT),
                    :,
                ]
        dims = (((1,), (1,)), ((), ()))
        peaks, lses, inverses = [], [], []
        blocks = PATCHES // BLOCK
        tops, totals = [None] * ITEMS, [None] * ITEMS

        def multiply(u, c):
            part = (mine_ref, other_ref)[c * BLOCK // HALF]
            first = c * BLOCK % HALF
            block = lax.dot_general(
                part[page[u], first : first + BLOCK, :], token_refs[u][...], dims,
                preferred_element_type=jnp.float32,
            )
            logit_refs[u][c * BLOCK : (c + 1) * BLOCK, :] = block
            top = jnp.max(block.reshape(BLOCK // 8, 8, rows), axis=0)
            tops[u] = top if c == 0 else jnp.maximum(tops[u], top)

        def raise_e(u, c):
            piece = logit_refs[u][c * BLOCK : (c + 1) * BLOCK, :]
            e = jnp.exp2(LOG2 * (piece - peaks[u]))
            expo_refs[u][c * BLOCK : (c + 1) * BLOCK, :] = e.astype(jnp.bfloat16)
            low = jnp.sum(e.reshape(BLOCK // 8, 8, rows), axis=0)
            totals[u] = low if c == 0 else totals[u] + low

        grads = []
        for c in range(blocks):
            multiply(0, c)
        for u in range(ITEMS):
            peaks.append(jnp.max(tops[u], axis=0, keepdims=True))
            for c in range(blocks):
                if u + 1 < ITEMS:
                    multiply(u + 1, c)
                raise_e(u, c)
            total = jnp.sum(totals[u], axis=0, keepdims=True)
            lse = SHARPNESS * peaks[u] + jnp.log(total)
            lses.append(jnp.broadcast_to(lse, (W, rows)).T)
            inverses.append(jnp.broadcast_to(1.0 / total, (W, rows)).T)
            grads.append(
                jnp.dot(turned[page[u]], expo_refs[u][...], preferred_element_type=jnp.float32).T
            )
        scale = []
        for u in range(ITEMS):
            page_id = first_page + column_ref[page[u]] * NY
            hot = jnp.logical_or(hot_ref[0] == page_id, hot_ref[1] == page_id)
            shift = jnp.where(hot, HOT_SHIFT, 0.0).astype(jnp.float32)
            parts = []
            for g in range(GROUP):
                mine = slice(g * QT, (g + 1) * QT)
                score = jnp.sum(lses[u][mine], axis=0, keepdims=True) / SHARPNESS
                logit = SLOPE_SCALE * score + offset - shift
                label = slot_label[base[u] + g].astype(jnp.float32)
                live = jnp.where(g < left[u], SLOPE_SCALE, 0.0)
                slope = live * (1.0 / (1.0 + jnp.exp(-logit)) - label)
                parts.append(slope * inverses[u][mine])
            scale.append(jnp.concatenate(parts, axis=0))
        for u in range(ITEMS):
            scaled = (token_refs[u][...].astype(jnp.float32) * scale[u]).astype(jnp.bfloat16)
            page_acc[page[u]] += jnp.dot(
                expo_refs[u][...], scaled, preferred_element_type=jnp.float32
            )
        for u in range(ITEMS):
            grad = grads[u] * scale[u]
            for g in range(GROUP):
                rows_at = pl.ds(pl.multiple_of(query[u][g] * QT, QT), QT)
                query_acc[rows_at, :] += grad[g * QT : (g + 1) * QT]
        return 0

    lax.fori_loop(0, (items + ITEMS - 1) // ITEMS, per_round, 0)
    for k in range(PART):
        mine_out[k] = page_acc[k, :HALF, :].astype(jnp.bfloat16)
        other_out[k] = page_acc[k, HALF:, :].astype(jnp.bfloat16)
    if query_out is not query_acc:
        query_out[...] = query_acc[...].astype(jnp.bfloat16)


def exchange(array, axes):
    return lax.all_to_all(array, axes, split_axis=0, concat_axis=0, tiled=True)


def swap_cores(array):
    return lax.ppermute(array, "core", [(0, 1), (1, 0)])


def move(array, step):
    return lax.ppermute(array, "z", [(i, (i + step) % NZ) for i in range(NZ)])


def gather_column(half):
    below, above, across = move(half, 1), move(half, -1), move(half, 4)
    far_below = move(jnp.stack([below, across]), 1)
    far_above = move(jnp.stack([above, across]), -1)
    return jnp.stack([half, below, above, across]), jnp.concatenate([far_below, far_above])


def add(mine, other):
    return mine.astype(jnp.float32) + other.astype(jnp.float32)


def reduce_column(mine, other, from_below, from_above):
    up = (add(mine[2], other[2]) + from_below[0].astype(jnp.float32)).astype(jnp.bfloat16)
    down = (add(mine[1], other[1]) + from_above[0].astype(jnp.float32)).astype(jnp.bfloat16)
    over = (add(mine[3], other[3]) + add(from_below[1], from_above[1])).astype(jnp.bfloat16)
    total = add(mine[0], other[0])
    for part in (move(up, 1), move(down, -1), move(over, 4)):
        total = total + part.astype(jnp.float32)
    return total.astype(jnp.bfloat16)


def first_kernel(offset, *refs):
    score_kernel(offset, *refs[:6], None, *refs[6:15], None, *refs[15:])


def second_kernel(offset, *refs):
    score_kernel(offset, *refs)


def score(column, hot_pages, table, got, mine, other, carried=None):
    offset = -SLOPE_SCALE * QT * (math.log(PATCHES) / SHARPNESS + SHARPNESS / 2.0)
    smem = pl.BlockSpec(memory_space=pltpu.SMEM)
    vmem = pl.BlockSpec(memory_space=pltpu.VMEM)
    last = carried is not None
    pages = jax.ShapeDtypeStruct((PART, HALF, W), jnp.bfloat16)
    sums = jax.ShapeDtypeStruct((PLANE * ROWS, W), jnp.bfloat16 if last else jnp.float32)
    items = PART * SLOTS // GROUP + ITEMS
    rows = GROUP * QT
    scratch = [
        pltpu.SMEM((PART * LIST + GROUP,), jnp.int32),
        pltpu.SMEM((PART * LIST + GROUP,), jnp.int32),
        pltpu.SMEM((items,), jnp.int32),
        pltpu.SMEM((items,), jnp.int32),
        pltpu.SMEM((items,), jnp.int32),
        pltpu.VMEM((PART, W, PATCHES), jnp.bfloat16),
    ]
    scratch += [pltpu.VMEM((PLANE * ROWS, W), jnp.float32)] * last
    scratch += [pltpu.VMEM((PART, PATCHES, W), jnp.float32)]
    scratch += [pltpu.VMEM((rows, W), jnp.bfloat16)] * ITEMS
    scratch += [pltpu.VMEM((PATCHES, rows), jnp.float32)] * ITEMS
    scratch += [pltpu.VMEM((PATCHES, rows), jnp.bfloat16)] * ITEMS
    return pl.pallas_call(
        functools.partial(second_kernel if last else first_kernel, offset),
        out_shape=(sums, pages, pages),
        in_specs=[smem] * 3 + [vmem] * (3 + last),
        out_specs=(vmem, vmem, vmem),
        scratch_shapes=scratch,
        compiler_params=pltpu.CompilerParams(vmem_limit_bytes=18 << 20),
        cost_estimate=pl.CostEstimate(
            flops=6 * PLANE * CAP * 2 * QT * PATCHES * W * 2,
            bytes_accessed=8 << 20,
            transcendentals=PLANE * CAP * 2 * QT * PATCHES,
        ),
    )(column, hot_pages, table, got, mine, other, *([carried] if last else []))


def shards(queries, pages, pair_page, pair_query, pair_label, hot_pages):
    smem = pl.BlockSpec(memory_space=pltpu.SMEM)
    vmem = pl.BlockSpec(memory_space=pltpu.VMEM)
    core = lax.axis_index("core").reshape(1)
    send, half = pl.pallas_call(
        pack_kernel,
        out_shape=(
            jax.ShapeDtypeStruct((PLANE, SEND_ROWS, W), jnp.bfloat16),
            jax.ShapeDtypeStruct((HALF, W), jnp.bfloat16),
        ),
        in_specs=[smem] * 4 + [vmem] * 2,
        out_specs=(vmem, vmem),
    )(pair_page[:, 0], pair_query, pair_label, core, queries.reshape(ROWS, W), pages[0])
    near, far = gather_column(half)
    other_near, other_far = swap_cores(near), swap_cores(far)
    got = exchange(send, ("x", "y"))
    table = got[:, ROWS, : 2 * ENTRIES].astype(jnp.int32)
    heights = (lax.axis_index("z") + jnp.array(STEPS, jnp.int32)) % NZ
    first_page = (lax.axis_index("x") * (NZ * NY) + lax.axis_index("y")).reshape(1)
    near_column = jnp.concatenate([heights[:PART], first_page])
    far_column = jnp.concatenate([heights[PART:], first_page])
    sums, far_mine, far_other = score(far_column, hot_pages, table, got, far, other_far)
    far_other = swap_cores(far_other)
    to_above = add(far_mine[2:4], far_other[2:4]).astype(jnp.bfloat16)
    to_below = add(far_mine[0:2], far_other[0:2]).astype(jnp.bfloat16)
    sums, to_above, to_below = lax.optimization_barrier((sums, to_above, to_below))
    from_below, from_above = move(to_above, 1), move(to_below, -1)
    query_part, near_mine, near_other = score(
        near_column, hot_pages, table, got, near, other_near, sums
    )
    near_other = swap_cores(near_other)
    query_part, from_below, from_above = lax.optimization_barrier(
        (query_part, from_below, from_above)
    )
    query_back = exchange(query_part.reshape(PLANE, ROWS, W), ("x", "y"))
    page_grad = reduce_column(near_mine, near_other, from_below, from_above)
    query_grad = jnp.sum(query_back.astype(jnp.float32), axis=0).astype(jnp.bfloat16)
    return query_grad.reshape(Q_DEV, QT, W), page_grad[None]


def solution(mesh):
    torus = Mesh(mesh.devices.reshape(NX, NZ, NY, NC), ("x", "z", "y", "core"))
    owner = ("x", "z", "y")
    device = ("x", "z", "y", "core")
    return jax.shard_map(
        shards,
        mesh=torus,
        in_specs=(P(device), P(owner), P(device), P(device), P(device), P()),
        out_specs=(P(device), P(owner, "core")),
        check_vma=False,
    )
```

```python
import functools
import math

import jax
import jax.numpy as jnp
from jax import lax
from jax.experimental import pallas as pl
from jax.experimental.pallas import tpu as pltpu
from jax.sharding import Mesh, PartitionSpec as P

SHARPNESS = 4.0
SLOPE_SCALE = 0.5
HOT_SHIFT = 2.0

NX, NZ, NY, NC = 4, 8, 4, 2
PLANE = NX * NY
QT = 32
W = 128
Q_DEV = 8
PAIR_DEV = 64
PATCHES = 1024
HALF = PATCHES // 2
CAP = 2
ROWS = Q_DEV * QT
SEND_ROWS = ROWS + 16
ENTRIES = NZ * CAP
GROUP = 8
BLOCK = 128
LOG2 = 4.0 * math.log2(math.e)
SLOTS = PLANE * CAP
LIST = SLOTS + GROUP
PART = NZ // 2
STEPS = (0, -1, 1, 4, -2, 3, 2, -3)


def pack_kernel(
    page_ref, query_ref, label_ref, core_ref, rows_ref, whole_ref, out_ref, half_ref, table_ref, done
):
    at = pl.ds(pl.multiple_of(core_ref[0] * HALF, HALF), HALF)
    copies = [pltpu.make_async_copy(whole_ref.at[at, :], half_ref, done.at[PLANE])]
    for d in range(PLANE):
        copies.append(
            pltpu.make_async_copy(rows_ref, out_ref.at[d, pl.ds(0, ROWS), :], done.at[d])
        )
    for copy in copies:
        copy.start()
    dest = lax.broadcasted_iota(jnp.int32, (PLANE, W), 0)
    lane = lax.broadcasted_iota(jnp.int32, (PLANE, W), 1)
    entry = lane % ENTRIES
    rank = entry % CAP
    wanted = (dest // NY) * (NZ * NY) + (entry // CAP) * NY + dest % NY
    is_query = lane < ENTRIES
    is_label = jnp.logical_and(lane >= ENTRIES, lane < 2 * ENTRIES)

    def visit(i, carry):
        table, seen = carry
        hit = wanted == page_ref[i]
        value = jnp.where(is_query, query_ref[i] + 1, jnp.where(is_label, label_ref[i], 0))
        table = jnp.where(jnp.logical_and(hit, seen == rank), value, table)
        return table, seen + hit.astype(jnp.int32)

    zeros = jnp.zeros((PLANE, W), jnp.int32)
    table, _ = lax.fori_loop(0, PAIR_DEV, visit, (zeros, zeros), unroll=8)
    table = table.astype(jnp.float32)
    for d in range(PLANE):
        table_ref[d] = jnp.broadcast_to(table[d : d + 1, :], (16, W)).astype(jnp.bfloat16)
    last = pltpu.make_async_copy(
        table_ref, out_ref.at[:, pl.ds(ROWS, SEND_ROWS - ROWS), :], done.at[PLANE + 1]
    )
    last.start()
    for copy in copies:
        copy.wait()
    last.wait()


def score_kernel(
    widths, offset, column_ref, hot_ref, table_ref, got_ref, mine_ref, other_ref, carried_ref,
    query_out, mine_out, other_out,
    slot_query, slot_label, item_page, item_base, item_left, turned, query_acc, page_acc, *work,
):
    rows = GROUP * QT
    if query_acc is None:
        query_acc = query_out
    most = max(widths)
    token_refs, logit_refs, expo_refs = work[:most], work[most : 2 * most], work[2 * most :]
    if carried_ref is None:
        query_acc[...] = jnp.zeros_like(query_acc)
    else:
        query_acc[...] = carried_ref[...]
    page_acc[...] = jnp.zeros_like(page_acc)
    first_page = column_ref[PART]

    def list_page(page, items):
        height = column_ref[page]
        turned[page, :, :HALF] = mine_ref[page].T
        turned[page, :, HALF:] = other_ref[page].T
        start = page * LIST
        count = jnp.int32(0)
        for s in range(PLANE):
            for r in range(CAP):
                code = table_ref[s, height * CAP + r]
                slot_query[start + count] = s * Q_DEV + code - 1
                slot_label[start + count] = table_ref[s, ENTRIES + height * CAP + r]
                count = count + (code > 0).astype(jnp.int32)
        for g in range(GROUP - 1):
            slot_query[start + count + g] = 0
            slot_label[start + count + g] = 0
        for j in range(SLOTS // GROUP):
            item_page[items] = page
            item_base[items] = start + j * GROUP
            item_left[items] = count - j * GROUP
            items = items + (count > j * GROUP).astype(jnp.int32)
        return items

    items = lax.fori_loop(0, PART, list_page, jnp.int32(0))
    for g in range(GROUP):
        slot_query[PART * LIST + g] = 0
        slot_label[PART * LIST + g] = 0
    for u in range(most):
        item_page[items + u] = 0
        item_base[items + u] = PART * LIST
        item_left[items + u] = 0

    def per_round(width, start, step, _):
        at = [start + step * width + u for u in range(width)]
        page = [item_page[i] for i in at]
        base = [item_base[i] for i in at]
        left = [item_left[i] for i in at]
        query = [[slot_query[b + g] for g in range(GROUP)] for b in base]
        for u in range(width):
            for g in range(GROUP):
                token_refs[u][g * QT : (g + 1) * QT, :] = got_ref[
                    lax.shift_right_logical(query[u][g], 3),
                    pl.ds(pl.multiple_of(lax.bitwise_and(query[u][g], Q_DEV - 1) * QT, QT), QT),
                    :,
                ]
        dims = (((1,), (1,)), ((), ()))
        peaks, lses, inverses = [], [], []
        blocks = PATCHES // BLOCK
        tops, totals = [None] * width, [None] * width

        def multiply(u, c):
            part = (mine_ref, other_ref)[c * BLOCK // HALF]
            first = c * BLOCK % HALF
            block = lax.dot_general(
                part[page[u], first : first + BLOCK, :], token_refs[u][...], dims,
                preferred_element_type=jnp.float32,
            )
            logit_refs[u][c * BLOCK : (c + 1) * BLOCK, :] = block
            top = jnp.max(block.reshape(BLOCK // 8, 8, rows), axis=0)
            tops[u] = top if c == 0 else jnp.maximum(tops[u], top)

        def raise_e(u, c):
            piece = logit_refs[u][c * BLOCK : (c + 1) * BLOCK, :]
            e = jnp.exp2(LOG2 * (piece - peaks[u]))
            expo_refs[u][c * BLOCK : (c + 1) * BLOCK, :] = e.astype(jnp.bfloat16)
            low = jnp.sum(e.reshape(BLOCK // 8, 8, rows), axis=0)
            totals[u] = low if c == 0 else totals[u] + low

        grads = []
        for c in range(blocks):
            multiply(0, c)
        for u in range(width):
            peaks.append(jnp.max(tops[u], axis=0, keepdims=True))
            for c in range(blocks):
                if u + 1 < width:
                    multiply(u + 1, c)
                raise_e(u, c)
            total = jnp.sum(totals[u], axis=0, keepdims=True)
            lse = SHARPNESS * peaks[u] + jnp.log(total)
            lses.append(jnp.broadcast_to(lse, (W, rows)).T)
            inverses.append(jnp.broadcast_to(1.0 / total, (W, rows)).T)
            grads.append(
                jnp.dot(turned[page[u]], expo_refs[u][...], preferred_element_type=jnp.float32).T
            )
        scale = []
        for u in range(width):
            page_id = first_page + column_ref[page[u]] * NY
            hot = jnp.logical_or(hot_ref[0] == page_id, hot_ref[1] == page_id)
            shift = jnp.where(hot, HOT_SHIFT, 0.0).astype(jnp.float32)
            parts = []
            for g in range(GROUP):
                mine = slice(g * QT, (g + 1) * QT)
                score = jnp.sum(lses[u][mine], axis=0, keepdims=True) / SHARPNESS
                logit = SLOPE_SCALE * score + offset - shift
                label = slot_label[base[u] + g].astype(jnp.float32)
                live = jnp.where(g < left[u], SLOPE_SCALE, 0.0)
                slope = live * (1.0 / (1.0 + jnp.exp(-logit)) - label)
                parts.append(slope * inverses[u][mine])
            scale.append(jnp.concatenate(parts, axis=0))
        for u in range(width):
            scaled = (token_refs[u][...].astype(jnp.float32) * scale[u]).astype(jnp.bfloat16)
            page_acc[page[u]] += jnp.dot(
                expo_refs[u][...], scaled, preferred_element_type=jnp.float32
            )
        for u in range(width):
            grad = grads[u] * scale[u]
            for g in range(GROUP):
                rows_at = pl.ds(pl.multiple_of(query[u][g] * QT, QT), QT)
                query_acc[rows_at, :] += grad[g * QT : (g + 1) * QT]
        return 0

    start = jnp.int32(0)
    for width in widths:
        if width == widths[-1]:
            turns = (items - start + width - 1) // width
        else:
            turns = (items - start + 1) // width
        lax.fori_loop(0, turns, functools.partial(per_round, width, start), 0)
        start = jnp.minimum(start + turns * width, items)
    for k in range(PART):
        mine_out[k] = page_acc[k, :HALF, :].astype(jnp.bfloat16)
        other_out[k] = page_acc[k, HALF:, :].astype(jnp.bfloat16)
    if query_out is not query_acc:
        query_out[...] = query_acc[...].astype(jnp.bfloat16)


def exchange(array, axes):
    return lax.all_to_all(array, axes, split_axis=0, concat_axis=0, tiled=True)


def swap_cores(array):
    return lax.ppermute(array, "core", [(0, 1), (1, 0)])


def move(array, step):
    return lax.ppermute(array, "z", [(i, (i + step) % NZ) for i in range(NZ)])


def gather_column(half):
    below, above, across = move(half, 1), move(half, -1), move(half, 4)
    far_below = move(jnp.stack([below, across]), 1)
    far_above = move(jnp.stack([above, across]), -1)
    return jnp.stack([half, below, above, across]), jnp.concatenate([far_below, far_above])


def add(mine, other):
    return mine.astype(jnp.float32) + other.astype(jnp.float32)


def reduce_column(mine, other, from_below, from_above):
    up = (add(mine[2], other[2]) + from_below[0].astype(jnp.float32)).astype(jnp.bfloat16)
    down = (add(mine[1], other[1]) + from_above[0].astype(jnp.float32)).astype(jnp.bfloat16)
    over = (add(mine[3], other[3]) + add(from_below[1], from_above[1])).astype(jnp.bfloat16)
    total = add(mine[0], other[0])
    for part in (move(up, 1), move(down, -1), move(over, 4)):
        total = total + part.astype(jnp.float32)
    return total.astype(jnp.bfloat16)


def first_kernel(widths, offset, *refs):
    score_kernel(widths, offset, *refs[:6], None, *refs[6:15], None, *refs[15:])


def second_kernel(widths, offset, *refs):
    score_kernel(widths, offset, *refs)


def score(column, hot_pages, table, got, mine, other, carried=None):
    offset = -SLOPE_SCALE * QT * (math.log(PATCHES) / SHARPNESS + SHARPNESS / 2.0)
    smem = pl.BlockSpec(memory_space=pltpu.SMEM)
    vmem = pl.BlockSpec(memory_space=pltpu.VMEM)
    last = carried is not None
    widths = (2,) if last else (4, 2)
    most = max(widths)
    pages = jax.ShapeDtypeStruct((PART, HALF, W), jnp.bfloat16)
    sums = jax.ShapeDtypeStruct((PLANE * ROWS, W), jnp.bfloat16 if last else jnp.float32)
    items = PART * SLOTS // GROUP + most
    rows = GROUP * QT
    scratch = [
        pltpu.SMEM((PART * LIST + GROUP,), jnp.int32),
        pltpu.SMEM((PART * LIST + GROUP,), jnp.int32),
        pltpu.SMEM((items,), jnp.int32),
        pltpu.SMEM((items,), jnp.int32),
        pltpu.SMEM((items,), jnp.int32),
        pltpu.VMEM((PART, W, PATCHES), jnp.bfloat16),
    ]
    scratch += [pltpu.VMEM((PLANE * ROWS, W), jnp.float32)] * last
    scratch += [pltpu.VMEM((PART, PATCHES, W), jnp.float32)]
    scratch += [pltpu.VMEM((rows, W), jnp.bfloat16)] * most
    scratch += [pltpu.VMEM((PATCHES, rows), jnp.float32)] * most
    scratch += [pltpu.VMEM((PATCHES, rows), jnp.bfloat16)] * most
    return pl.pallas_call(
        functools.partial(second_kernel if last else first_kernel, widths, offset),
        out_shape=(sums, pages, pages),
        in_specs=[smem] * 3 + [vmem] * (3 + last),
        out_specs=(vmem, vmem, vmem),
        scratch_shapes=scratch,
        compiler_params=pltpu.CompilerParams(vmem_limit_bytes=20 << 20),
        cost_estimate=pl.CostEstimate(
            flops=6 * PLANE * CAP * 2 * QT * PATCHES * W * 2,
            bytes_accessed=8 << 20,
            transcendentals=PLANE * CAP * 2 * QT * PATCHES,
        ),
    )(column, hot_pages, table, got, mine, other, *([carried] if last else []))


def shards(queries, pages, pair_page, pair_query, pair_label, hot_pages):
    smem = pl.BlockSpec(memory_space=pltpu.SMEM)
    vmem = pl.BlockSpec(memory_space=pltpu.VMEM)
    core = lax.axis_index("core").reshape(1)
    send, half = pl.pallas_call(
        pack_kernel,
        out_shape=(
            jax.ShapeDtypeStruct((PLANE, SEND_ROWS, W), jnp.bfloat16),
            jax.ShapeDtypeStruct((HALF, W), jnp.bfloat16),
        ),
        in_specs=[smem] * 4 + [pl.BlockSpec(memory_space=pl.ANY)] * 2,
        out_specs=(pl.BlockSpec(memory_space=pl.ANY),) * 2,
        scratch_shapes=[
            pltpu.VMEM((PLANE, SEND_ROWS - ROWS, W), jnp.bfloat16),
            pltpu.SemaphoreType.DMA((PLANE + 2,)),
        ],
    )(pair_page[:, 0], pair_query, pair_label, core, queries.reshape(ROWS, W), pages[0])
    near, far = gather_column(half)
    other_near, other_far = swap_cores(near), swap_cores(far)
    got = exchange(send, ("x", "y"))
    table = got[:, ROWS, : 2 * ENTRIES].astype(jnp.int32)
    heights = (lax.axis_index("z") + jnp.array(STEPS, jnp.int32)) % NZ
    first_page = (lax.axis_index("x") * (NZ * NY) + lax.axis_index("y")).reshape(1)
    near_column = jnp.concatenate([heights[:PART], first_page])
    far_column = jnp.concatenate([heights[PART:], first_page])
    sums, far_mine, far_other = score(far_column, hot_pages, table, got, far, other_far)
    far_other = swap_cores(far_other)
    to_above = add(far_mine[2:4], far_other[2:4]).astype(jnp.bfloat16)
    to_below = add(far_mine[0:2], far_other[0:2]).astype(jnp.bfloat16)
    sums, to_above, to_below = lax.optimization_barrier((sums, to_above, to_below))
    from_below, from_above = move(to_above, 1), move(to_below, -1)
    query_part, near_mine, near_other = score(
        near_column, hot_pages, table, got, near, other_near, sums
    )
    near_other = swap_cores(near_other)
    query_part, from_below, from_above = lax.optimization_barrier(
        (query_part, from_below, from_above)
    )
    query_back = exchange(query_part.reshape(PLANE, ROWS, W), ("x", "y"))
    page_grad = reduce_column(near_mine, near_other, from_below, from_above)
    query_grad = jnp.sum(query_back.astype(jnp.float32), axis=0).astype(jnp.bfloat16)
    return query_grad.reshape(Q_DEV, QT, W), page_grad[None]


def solution(mesh):
    torus = Mesh(mesh.devices.reshape(NX, NZ, NY, NC), ("x", "z", "y", "core"))
    owner = ("x", "z", "y")
    device = ("x", "z", "y", "core")
    return jax.shard_map(
        shards,
        mesh=torus,
        in_specs=(P(device), P(owner), P(device), P(device), P(device), P()),
        out_specs=(P(device), P(owner, "core")),
        check_vma=False,
    )
```

```python
import functools
import math

import jax
import jax.numpy as jnp
from jax import lax
from jax.experimental import pallas as pl
from jax.experimental.pallas import tpu as pltpu
from jax.sharding import Mesh, PartitionSpec as P

SHARPNESS = 4.0
SLOPE_SCALE = 0.5
HOT_SHIFT = 2.0

NX, NZ, NY, NC = 4, 8, 4, 2
PLANE = NX * NY
QT = 32
W = 128
Q_DEV = 8
PAIR_DEV = 64
PATCHES = 1024
HALF = PATCHES // 2
CAP = 2
ROWS = Q_DEV * QT
SEND_ROWS = ROWS + 16
ENTRIES = NZ * CAP
GROUP = 8
BLOCK = 128
LOG2 = 4.0 * math.log2(math.e)
SLOTS = PLANE * CAP
LIST = SLOTS + GROUP
PART = NZ // 2
STEPS = (0, -1, 1, 4, -2, 3, 2, -3)


def pack_kernel(
    page_ref, query_ref, label_ref, core_ref, rows_ref, whole_ref, out_ref, half_ref, table_ref, done
):
    at = pl.ds(pl.multiple_of(core_ref[0] * HALF, HALF), HALF)
    copies = [pltpu.make_async_copy(whole_ref.at[at, :], half_ref, done.at[PLANE])]
    for d in range(PLANE):
        copies.append(
            pltpu.make_async_copy(rows_ref, out_ref.at[d, pl.ds(0, ROWS), :], done.at[d])
        )
    for copy in copies:
        copy.start()
    dest = lax.broadcasted_iota(jnp.int32, (PLANE, W), 0)
    lane = lax.broadcasted_iota(jnp.int32, (PLANE, W), 1)
    entry = lane % ENTRIES
    rank = entry % CAP
    wanted = (dest // NY) * (NZ * NY) + (entry // CAP) * NY + dest % NY
    is_query = lane < ENTRIES
    is_label = jnp.logical_and(lane >= ENTRIES, lane < 2 * ENTRIES)

    def visit(i, carry):
        table, seen = carry
        hit = wanted == page_ref[i]
        value = jnp.where(is_query, query_ref[i] + 1, jnp.where(is_label, label_ref[i], 0))
        table = jnp.where(jnp.logical_and(hit, seen == rank), value, table)
        return table, seen + hit.astype(jnp.int32)

    zeros = jnp.zeros((PLANE, W), jnp.int32)
    table, _ = lax.fori_loop(0, PAIR_DEV, visit, (zeros, zeros), unroll=8)
    table = table.astype(jnp.float32)
    for d in range(PLANE):
        table_ref[d] = jnp.broadcast_to(table[d : d + 1, :], (16, W)).astype(jnp.bfloat16)
    last = pltpu.make_async_copy(
        table_ref, out_ref.at[:, pl.ds(ROWS, SEND_ROWS - ROWS), :], done.at[PLANE + 1]
    )
    last.start()
    for copy in copies:
        copy.wait()
    last.wait()


def score_kernel(
    widths, offset, column_ref, hot_ref, table_ref, got_ref, mine_ref, other_ref, carried_ref,
    query_out, mine_out, other_out,
    slot_query, slot_label, item_page, item_base, item_left, turned, query_acc, page_acc, *work,
):
    rows = GROUP * QT
    if query_acc is None:
        query_acc = query_out
    most = max(widths)
    token_refs, logit_refs, expo_refs = work[:most], work[most : 2 * most], work[2 * most :]
    if carried_ref is None:
        query_acc[...] = jnp.zeros_like(query_acc)
    else:
        query_acc[...] = carried_ref[...]
    page_acc[...] = jnp.zeros_like(page_acc)
    first_page = column_ref[PART]

    def list_page(page, items):
        height = column_ref[page]
        turned[page, :, :HALF] = mine_ref[page].T
        turned[page, :, HALF:] = other_ref[page].T
        start = page * LIST
        count = jnp.int32(0)
        for s in range(PLANE):
            for r in range(CAP):
                code = table_ref[s, height * CAP + r]
                slot_query[start + count] = s * Q_DEV + code - 1
                slot_label[start + count] = table_ref[s, ENTRIES + height * CAP + r]
                count = count + (code > 0).astype(jnp.int32)
        for g in range(GROUP - 1):
            slot_query[start + count + g] = 0
            slot_label[start + count + g] = 0
        for j in range(SLOTS // GROUP):
            item_page[items] = page
            item_base[items] = start + j * GROUP
            item_left[items] = count - j * GROUP
            items = items + (count > j * GROUP).astype(jnp.int32)
        return items

    items = lax.fori_loop(0, PART, list_page, jnp.int32(0))
    for g in range(GROUP):
        slot_query[PART * LIST + g] = 0
        slot_label[PART * LIST + g] = 0
    for u in range(most):
        item_page[items + u] = 0
        item_base[items + u] = PART * LIST
        item_left[items + u] = 0

    def per_round(width, start, step, _):
        at = [start + step * width + u for u in range(width)]
        page = [item_page[i] for i in at]
        base = [item_base[i] for i in at]
        left = [item_left[i] for i in at]
        query = [[slot_query[b + g] for g in range(GROUP)] for b in base]
        for u in range(width):
            for g in range(GROUP):
                token_refs[u][g * QT : (g + 1) * QT, :] = got_ref[
                    lax.shift_right_logical(query[u][g], 3),
                    pl.ds(pl.multiple_of(lax.bitwise_and(query[u][g], Q_DEV - 1) * QT, QT), QT),
                    :,
                ]
        dims = (((1,), (1,)), ((), ()))
        peaks, lses, inverses = [], [], []
        blocks = PATCHES // BLOCK
        tops, totals = [None] * width, [None] * width

        def multiply(u, c):
            part = (mine_ref, other_ref)[c * BLOCK // HALF]
            first = c * BLOCK % HALF
            block = lax.dot_general(
                part[page[u], first : first + BLOCK, :], token_refs[u][...], dims,
                preferred_element_type=jnp.float32,
            )
            logit_refs[u][c * BLOCK : (c + 1) * BLOCK, :] = block
            top = jnp.max(block.reshape(BLOCK // 8, 8, rows), axis=0)
            tops[u] = top if c == 0 else jnp.maximum(tops[u], top)

        def raise_e(u, c):
            piece = logit_refs[u][c * BLOCK : (c + 1) * BLOCK, :]
            e = jnp.exp2(LOG2 * (piece - peaks[u]))
            expo_refs[u][c * BLOCK : (c + 1) * BLOCK, :] = e.astype(jnp.bfloat16)
            low = jnp.sum(e.reshape(BLOCK // 8, 8, rows), axis=0)
            totals[u] = low if c == 0 else totals[u] + low

        grads = []
        for c in range(blocks):
            multiply(0, c)
        for u in range(width):
            peaks.append(jnp.max(tops[u], axis=0, keepdims=True))
            for c in range(blocks):
                if u + 1 < width:
                    multiply(u + 1, c)
                raise_e(u, c)
            total = jnp.sum(totals[u], axis=0, keepdims=True)
            lse = SHARPNESS * peaks[u] + jnp.log(total)
            lses.append(jnp.broadcast_to(lse, (W, rows)).T)
            inverses.append(jnp.broadcast_to(1.0 / total, (W, rows)).T)
            grads.append(
                jnp.dot(turned[page[u]], expo_refs[u][...], preferred_element_type=jnp.float32).T
            )
        scale = []
        for u in range(width):
            page_id = first_page + column_ref[page[u]] * NY
            hot = jnp.logical_or(hot_ref[0] == page_id, hot_ref[1] == page_id)
            shift = jnp.where(hot, HOT_SHIFT, 0.0).astype(jnp.float32)
            parts = []
            for g in range(GROUP):
                mine = slice(g * QT, (g + 1) * QT)
                score = jnp.sum(lses[u][mine], axis=0, keepdims=True) / SHARPNESS
                logit = SLOPE_SCALE * score + offset - shift
                label = slot_label[base[u] + g].astype(jnp.float32)
                live = jnp.where(g < left[u], SLOPE_SCALE, 0.0)
                slope = live * (1.0 / (1.0 + jnp.exp(-logit)) - label)
                parts.append(slope * inverses[u][mine])
            scale.append(jnp.concatenate(parts, axis=0))
        for u in range(width):
            scaled = (token_refs[u][...].astype(jnp.float32) * scale[u]).astype(jnp.bfloat16)
            page_acc[page[u]] += jnp.dot(
                expo_refs[u][...], scaled, preferred_element_type=jnp.float32
            )
        for u in range(width):
            grad = grads[u] * scale[u]
            for g in range(GROUP):
                rows_at = pl.ds(pl.multiple_of(query[u][g] * QT, QT), QT)
                query_acc[rows_at, :] += grad[g * QT : (g + 1) * QT]
        return 0

    start = jnp.int32(0)
    for width in widths:
        if width == widths[-1]:
            turns = (items - start + width - 1) // width
        else:
            turns = (items - start + 1) // width
        lax.fori_loop(0, turns, functools.partial(per_round, width, start), 0)
        start = jnp.minimum(start + turns * width, items)
    for k in range(PART):
        mine_out[k] = page_acc[k, :HALF, :].astype(jnp.bfloat16)
        other_out[k] = page_acc[k, HALF:, :].astype(jnp.bfloat16)
    if query_out is not query_acc:
        query_out[...] = query_acc[...].astype(jnp.bfloat16)


def exchange(array, axes):
    return lax.all_to_all(array, axes, split_axis=0, concat_axis=0, tiled=True)


def swap_cores(array):
    return lax.ppermute(array, "core", [(0, 1), (1, 0)])


def move(array, step):
    return lax.ppermute(array, "z", [(i, (i + step) % NZ) for i in range(NZ)])


def gather_column(half):
    below, above, across = move(half, 1), move(half, -1), move(half, 4)
    far_below = move(jnp.stack([below, across]), 1)
    far_above = move(jnp.stack([above, across]), -1)
    return jnp.stack([half, below, above, across]), jnp.concatenate([far_below, far_above])


def add(mine, other):
    return mine.astype(jnp.float32) + other.astype(jnp.float32)


def reduce_column(mine, other, from_below, from_above):
    up = (add(mine[2], other[2]) + from_below[0].astype(jnp.float32)).astype(jnp.bfloat16)
    down = (add(mine[1], other[1]) + from_above[0].astype(jnp.float32)).astype(jnp.bfloat16)
    over = (add(mine[3], other[3]) + add(from_below[1], from_above[1])).astype(jnp.bfloat16)
    total = add(mine[0], other[0])
    for part in (move(up, 1), move(down, -1), move(over, 4)):
        total = total + part.astype(jnp.float32)
    return total.astype(jnp.bfloat16)


def first_kernel(widths, offset, *refs):
    score_kernel(widths, offset, *refs[:6], None, *refs[6:15], None, *refs[15:])


def second_kernel(widths, offset, *refs):
    score_kernel(widths, offset, *refs)


def score(column, hot_pages, table, got, mine, other, carried=None):
    offset = -SLOPE_SCALE * QT * (math.log(PATCHES) / SHARPNESS + SHARPNESS / 2.0)
    smem = pl.BlockSpec(memory_space=pltpu.SMEM)
    vmem = pl.BlockSpec(memory_space=pltpu.VMEM)
    last = carried is not None
    widths = (2,) if last else (4, 2)
    most = max(widths)
    pages = jax.ShapeDtypeStruct((PART, HALF, W), jnp.bfloat16)
    sums = jax.ShapeDtypeStruct((PLANE * ROWS, W), jnp.bfloat16 if last else jnp.float32)
    items = PART * SLOTS // GROUP + most
    rows = GROUP * QT
    scratch = [
        pltpu.SMEM((PART * LIST + GROUP,), jnp.int32),
        pltpu.SMEM((PART * LIST + GROUP,), jnp.int32),
        pltpu.SMEM((items,), jnp.int32),
        pltpu.SMEM((items,), jnp.int32),
        pltpu.SMEM((items,), jnp.int32),
        pltpu.VMEM((PART, W, PATCHES), jnp.bfloat16),
    ]
    scratch += [pltpu.VMEM((PLANE * ROWS, W), jnp.float32)] * last
    scratch += [pltpu.VMEM((PART, PATCHES, W), jnp.float32)]
    scratch += [pltpu.VMEM((rows, W), jnp.bfloat16)] * most
    scratch += [pltpu.VMEM((PATCHES, rows), jnp.float32)] * most
    scratch += [pltpu.VMEM((PATCHES, rows), jnp.bfloat16)] * most
    return pl.pallas_call(
        functools.partial(second_kernel if last else first_kernel, widths, offset),
        out_shape=(sums, pages, pages),
        in_specs=[smem] * 3 + [vmem] * (3 + last),
        out_specs=(vmem, vmem, vmem),
        scratch_shapes=scratch,
        compiler_params=pltpu.CompilerParams(vmem_limit_bytes=20 << 20),
        cost_estimate=pl.CostEstimate(
            flops=6 * PLANE * CAP * 2 * QT * PATCHES * W * 2,
            bytes_accessed=8 << 20,
            transcendentals=PLANE * CAP * 2 * QT * PATCHES,
        ),
    )(column, hot_pages, table, got, mine, other, *([carried] if last else []))


def shards(queries, pages, pair_page, pair_query, pair_label, hot_pages):
    smem = pl.BlockSpec(memory_space=pltpu.SMEM)
    vmem = pl.BlockSpec(memory_space=pltpu.VMEM)
    core = lax.axis_index("core").reshape(1)
    send, half = pl.pallas_call(
        pack_kernel,
        out_shape=(
            jax.ShapeDtypeStruct((PLANE, SEND_ROWS, W), jnp.bfloat16),
            jax.ShapeDtypeStruct((HALF, W), jnp.bfloat16),
        ),
        in_specs=[smem] * 4 + [vmem] * 2,
        out_specs=(pl.BlockSpec(memory_space=pl.ANY),) * 2,
        scratch_shapes=[
            pltpu.VMEM((PLANE, SEND_ROWS - ROWS, W), jnp.bfloat16),
            pltpu.SemaphoreType.DMA((PLANE + 2,)),
        ],
    )(pair_page[:, 0], pair_query, pair_label, core, queries.reshape(ROWS, W), pages[0])
    near, far = gather_column(half)
    other_near, other_far = swap_cores(near), swap_cores(far)
    got = exchange(send, ("x", "y"))
    table = got[:, ROWS, : 2 * ENTRIES].astype(jnp.int32)
    heights = (lax.axis_index("z") + jnp.array(STEPS, jnp.int32)) % NZ
    first_page = (lax.axis_index("x") * (NZ * NY) + lax.axis_index("y")).reshape(1)
    near_column = jnp.concatenate([heights[:PART], first_page])
    far_column = jnp.concatenate([heights[PART:], first_page])
    sums, far_mine, far_other = score(far_column, hot_pages, table, got, far, other_far)
    far_other = swap_cores(far_other)
    to_above = add(far_mine[2:4], far_other[2:4]).astype(jnp.bfloat16)
    to_below = add(far_mine[0:2], far_other[0:2]).astype(jnp.bfloat16)
    sums, to_above, to_below = lax.optimization_barrier((sums, to_above, to_below))
    from_below, from_above = move(to_above, 1), move(to_below, -1)
    query_part, near_mine, near_other = score(
        near_column, hot_pages, table, got, near, other_near, sums
    )
    near_other = swap_cores(near_other)
    query_part, from_below, from_above = lax.optimization_barrier(
        (query_part, from_below, from_above)
    )
    query_back = exchange(query_part.reshape(PLANE, ROWS, W), ("x", "y"))
    page_grad = reduce_column(near_mine, near_other, from_below, from_above)
    query_grad = jnp.sum(query_back.astype(jnp.float32), axis=0).astype(jnp.bfloat16)
    return query_grad.reshape(Q_DEV, QT, W), page_grad[None]


def solution(mesh):
    torus = Mesh(mesh.devices.reshape(NX, NZ, NY, NC), ("x", "z", "y", "core"))
    owner = ("x", "z", "y")
    device = ("x", "z", "y", "core")
    return jax.shard_map(
        shards,
        mesh=torus,
        in_specs=(P(device), P(owner), P(device), P(device), P(device), P()),
        out_specs=(P(device), P(owner, "core")),
        check_vma=False,
    )
```

```python
import functools
import math

import jax
import jax.numpy as jnp
from jax import lax
from jax.experimental import pallas as pl
from jax.experimental.pallas import tpu as pltpu
from jax.sharding import Mesh, PartitionSpec as P

SHARPNESS = 4.0
SLOPE_SCALE = 0.5
HOT_SHIFT = 2.0

NX, NZ, NY, NC = 4, 8, 4, 2
PLANE = NX * NY
QT = 32
W = 128
Q_DEV = 8
PAIR_DEV = 64
PATCHES = 1024
HALF = PATCHES // 2
CAP = 2
ROWS = Q_DEV * QT
SEND_ROWS = ROWS + 16
ENTRIES = NZ * CAP
GROUP = 8
BLOCK = 128
LOG2 = 4.0 * math.log2(math.e)
SLOTS = PLANE * CAP
LIST = SLOTS + GROUP
PART = NZ // 2
COMBINE_FLOPS = 40 * 10**9
STEPS = (0, -1, 1, 4, -2, 3, 2, -3)


def pack_kernel(
    page_ref, query_ref, label_ref, core_ref, rows_ref, whole_ref, out_ref, half_ref, table_ref, done
):
    at = pl.ds(pl.multiple_of(core_ref[0] * HALF, HALF), HALF)
    copies = [pltpu.make_async_copy(whole_ref.at[at, :], half_ref, done.at[PLANE])]
    for d in range(PLANE):
        copies.append(
            pltpu.make_async_copy(rows_ref, out_ref.at[d, pl.ds(0, ROWS), :], done.at[d])
        )
    for copy in copies:
        copy.start()
    dest = lax.broadcasted_iota(jnp.int32, (PLANE, W), 0)
    lane = lax.broadcasted_iota(jnp.int32, (PLANE, W), 1)
    entry = lane % ENTRIES
    rank = entry % CAP
    wanted = (dest // NY) * (NZ * NY) + (entry // CAP) * NY + dest % NY
    is_query = lane < ENTRIES
    is_label = jnp.logical_and(lane >= ENTRIES, lane < 2 * ENTRIES)

    def visit(i, carry):
        table, seen = carry
        hit = wanted == page_ref[i]
        value = jnp.where(is_query, query_ref[i] + 1, jnp.where(is_label, label_ref[i], 0))
        table = jnp.where(jnp.logical_and(hit, seen == rank), value, table)
        return table, seen + hit.astype(jnp.int32)

    zeros = jnp.zeros((PLANE, W), jnp.int32)
    table, _ = lax.fori_loop(0, PAIR_DEV, visit, (zeros, zeros), unroll=8)
    table = table.astype(jnp.float32)
    for d in range(PLANE):
        table_ref[d] = jnp.broadcast_to(table[d : d + 1, :], (16, W)).astype(jnp.bfloat16)
    last = pltpu.make_async_copy(
        table_ref, out_ref.at[:, pl.ds(ROWS, SEND_ROWS - ROWS), :], done.at[PLANE + 1]
    )
    last.start()
    for copy in copies:
        copy.wait()
    last.wait()


def score_kernel(
    widths, offset, column_ref, hot_ref, table_ref, got_ref, mine_ref, other_ref, carried_ref,
    query_out, mine_out, other_out,
    slot_query, slot_label, item_page, item_base, item_left, turned, query_acc, page_acc, *work,
):
    rows = GROUP * QT
    if query_acc is None:
        query_acc = query_out
    most = max(widths)
    token_refs, logit_refs, expo_refs = work[:most], work[most : 2 * most], work[2 * most :]
    if carried_ref is None:
        query_acc[...] = jnp.zeros_like(query_acc)
    else:
        query_acc[...] = carried_ref[...]
    page_acc[...] = jnp.zeros_like(page_acc)
    first_page = column_ref[PART]

    def list_page(page, items):
        height = column_ref[page]
        turned[page, :, :HALF] = mine_ref[page].T
        turned[page, :, HALF:] = other_ref[page].T
        start = page * LIST
        count = jnp.int32(0)
        for s in range(PLANE):
            for r in range(CAP):
                code = table_ref[s, height * CAP + r]
                slot_query[start + count] = s * Q_DEV + code - 1
                slot_label[start + count] = table_ref[s, ENTRIES + height * CAP + r]
                count = count + (code > 0).astype(jnp.int32)
        for g in range(GROUP - 1):
            slot_query[start + count + g] = 0
            slot_label[start + count + g] = 0
        for j in range(SLOTS // GROUP):
            item_page[items] = page
            item_base[items] = start + j * GROUP
            item_left[items] = count - j * GROUP
            items = items + (count > j * GROUP).astype(jnp.int32)
        return items

    items = lax.fori_loop(0, PART, list_page, jnp.int32(0))
    for g in range(GROUP):
        slot_query[PART * LIST + g] = 0
        slot_label[PART * LIST + g] = 0
    for u in range(most):
        item_page[items + u] = 0
        item_base[items + u] = PART * LIST
        item_left[items + u] = 0

    def per_round(width, start, step, _):
        at = [start + step * width + u for u in range(width)]
        page = [item_page[i] for i in at]
        base = [item_base[i] for i in at]
        left = [item_left[i] for i in at]
        query = [[slot_query[b + g] for g in range(GROUP)] for b in base]
        for u in range(width):
            for g in range(GROUP):
                token_refs[u][g * QT : (g + 1) * QT, :] = got_ref[
                    lax.shift_right_logical(query[u][g], 3),
                    pl.ds(pl.multiple_of(lax.bitwise_and(query[u][g], Q_DEV - 1) * QT, QT), QT),
                    :,
                ]
        dims = (((1,), (1,)), ((), ()))
        peaks, lses, inverses = [], [], []
        blocks = PATCHES // BLOCK
        tops, totals = [None] * width, [None] * width

        def multiply(u, c):
            part = (mine_ref, other_ref)[c * BLOCK // HALF]
            first = c * BLOCK % HALF
            block = lax.dot_general(
                part[page[u], first : first + BLOCK, :], token_refs[u][...], dims,
                preferred_element_type=jnp.float32,
            )
            logit_refs[u][c * BLOCK : (c + 1) * BLOCK, :] = block
            top = jnp.max(block.reshape(BLOCK // 8, 8, rows), axis=0)
            tops[u] = top if c == 0 else jnp.maximum(tops[u], top)

        def raise_e(u, c):
            piece = logit_refs[u][c * BLOCK : (c + 1) * BLOCK, :]
            e = jnp.exp2(LOG2 * (piece - peaks[u]))
            expo_refs[u][c * BLOCK : (c + 1) * BLOCK, :] = e.astype(jnp.bfloat16)
            low = jnp.sum(e.reshape(BLOCK // 8, 8, rows), axis=0)
            totals[u] = low if c == 0 else totals[u] + low

        grads = []
        for c in range(blocks):
            multiply(0, c)
        for u in range(width):
            peaks.append(jnp.max(tops[u], axis=0, keepdims=True))
            for c in range(blocks):
                if u + 1 < width:
                    multiply(u + 1, c)
                raise_e(u, c)
            total = jnp.sum(totals[u], axis=0, keepdims=True)
            lse = SHARPNESS * peaks[u] + jnp.log(total)
            lses.append(jnp.broadcast_to(lse, (W, rows)).T)
            inverses.append(jnp.broadcast_to(1.0 / total, (W, rows)).T)
            grads.append(
                jnp.dot(turned[page[u]], expo_refs[u][...], preferred_element_type=jnp.float32).T
            )
        scale = []
        for u in range(width):
            page_id = first_page + column_ref[page[u]] * NY
            hot = jnp.logical_or(hot_ref[0] == page_id, hot_ref[1] == page_id)
            shift = jnp.where(hot, HOT_SHIFT, 0.0).astype(jnp.float32)
            parts = []
            for g in range(GROUP):
                mine = slice(g * QT, (g + 1) * QT)
                score = jnp.sum(lses[u][mine], axis=0, keepdims=True) / SHARPNESS
                logit = SLOPE_SCALE * score + offset - shift
                label = slot_label[base[u] + g].astype(jnp.float32)
                live = jnp.where(g < left[u], SLOPE_SCALE, 0.0)
                slope = live * (1.0 / (1.0 + jnp.exp(-logit)) - label)
                parts.append(slope * inverses[u][mine])
            scale.append(jnp.concatenate(parts, axis=0))
        for u in range(width):
            scaled = (token_refs[u][...].astype(jnp.float32) * scale[u]).astype(jnp.bfloat16)
            page_acc[page[u]] += jnp.dot(
                expo_refs[u][...], scaled, preferred_element_type=jnp.float32
            )
        for u in range(width):
            grad = grads[u] * scale[u]
            for g in range(GROUP):
                rows_at = pl.ds(pl.multiple_of(query[u][g] * QT, QT), QT)
                query_acc[rows_at, :] += grad[g * QT : (g + 1) * QT]
        return 0

    start = jnp.int32(0)
    for width in widths:
        if width == widths[-1]:
            turns = (items - start + width - 1) // width
        else:
            turns = (items - start + 1) // width
        lax.fori_loop(0, turns, functools.partial(per_round, width, start), 0)
        start = jnp.minimum(start + turns * width, items)
    for k in range(PART):
        mine_out[k] = page_acc[k, :HALF, :].astype(jnp.bfloat16)
        other_out[k] = page_acc[k, HALF:, :].astype(jnp.bfloat16)
    if query_out is not query_acc:
        query_out[...] = query_acc[...].astype(jnp.bfloat16)


def exchange(array, axes):
    return lax.all_to_all(array, axes, split_axis=0, concat_axis=0, tiled=True)


def swap_cores(array):
    return lax.ppermute(array, "core", [(0, 1), (1, 0)])


def move(array, step):
    return lax.ppermute(array, "z", [(i, (i + step) % NZ) for i in range(NZ)])


def gather_column(half):
    below, above, across = move(half, 1), move(half, -1), move(half, 4)
    far_below = move(jnp.stack([below, across]), 1)
    far_above = move(jnp.stack([above, across]), -1)
    return jnp.stack([half, below, above, across]), jnp.concatenate([far_below, far_above])


def add(mine, other):
    return mine.astype(jnp.float32) + other.astype(jnp.float32)


def combine_kernel(mine_ref, other_ref, below_ref, above_ref, up_ref, down_ref, over_ref):
    below, above = below_ref[...].astype(jnp.float32), above_ref[...].astype(jnp.float32)
    up_ref[...] = (add(mine_ref[2], other_ref[2]) + below[0]).astype(jnp.bfloat16)
    down_ref[...] = (add(mine_ref[1], other_ref[1]) + above[0]).astype(jnp.bfloat16)
    over_ref[...] = (add(mine_ref[3], other_ref[3]) + below[1] + above[1]).astype(jnp.bfloat16)


def reduce_column(mine, other, from_below, from_above):
    vmem = pl.BlockSpec(memory_space=pltpu.VMEM)
    up, down, over = pl.pallas_call(
        combine_kernel,
        out_shape=(jax.ShapeDtypeStruct((HALF, W), jnp.bfloat16),) * 3,
        in_specs=[vmem] * 4,
        out_specs=(vmem,) * 3,
        compiler_params=pltpu.CompilerParams(vmem_limit_bytes=6 << 20),
        cost_estimate=pl.CostEstimate(
            flops=COMBINE_FLOPS, bytes_accessed=4 << 20, transcendentals=0
        ),
    )(mine, other, from_below, from_above)
    total = add(mine[0], other[0])
    for part in (move(up, 1), move(down, -1), move(over, 4)):
        total = total + part.astype(jnp.float32)
    return total.astype(jnp.bfloat16)


def first_kernel(widths, offset, *refs):
    score_kernel(widths, offset, *refs[:6], None, *refs[6:15], None, *refs[15:])


def second_kernel(widths, offset, *refs):
    score_kernel(widths, offset, *refs)


def score(column, hot_pages, table, got, mine, other, carried=None):
    offset = -SLOPE_SCALE * QT * (math.log(PATCHES) / SHARPNESS + SHARPNESS / 2.0)
    smem = pl.BlockSpec(memory_space=pltpu.SMEM)
    vmem = pl.BlockSpec(memory_space=pltpu.VMEM)
    last = carried is not None
    widths = (4, 2)
    most = max(widths)
    pages = jax.ShapeDtypeStruct((PART, HALF, W), jnp.bfloat16)
    sums = jax.ShapeDtypeStruct((PLANE * ROWS, W), jnp.bfloat16 if last else jnp.float32)
    items = PART * SLOTS // GROUP + most
    rows = GROUP * QT
    scratch = [
        pltpu.SMEM((PART * LIST + GROUP,), jnp.int32),
        pltpu.SMEM((PART * LIST + GROUP,), jnp.int32),
        pltpu.SMEM((items,), jnp.int32),
        pltpu.SMEM((items,), jnp.int32),
        pltpu.SMEM((items,), jnp.int32),
        pltpu.VMEM((PART, W, PATCHES), jnp.bfloat16),
    ]
    scratch += [pltpu.VMEM((PLANE * ROWS, W), jnp.float32)] * last
    scratch += [pltpu.VMEM((PART, PATCHES, W), jnp.float32)]
    scratch += [pltpu.VMEM((rows, W), jnp.bfloat16)] * most
    scratch += [pltpu.VMEM((PATCHES, rows), jnp.float32)] * most
    scratch += [pltpu.VMEM((PATCHES, rows), jnp.bfloat16)] * most
    return pl.pallas_call(
        functools.partial(second_kernel if last else first_kernel, widths, offset),
        out_shape=(sums, pages, pages),
        in_specs=[smem] * 3 + [vmem] * (3 + last),
        out_specs=(vmem, vmem, vmem),
        scratch_shapes=scratch,
        compiler_params=pltpu.CompilerParams(vmem_limit_bytes=20 << 20),
        cost_estimate=pl.CostEstimate(
            flops=6 * PLANE * CAP * 2 * QT * PATCHES * W * 2,
            bytes_accessed=8 << 20,
            transcendentals=PLANE * CAP * 2 * QT * PATCHES,
        ),
    )(column, hot_pages, table, got, mine, other, *([carried] if last else []))


def shards(queries, pages, pair_page, pair_query, pair_label, hot_pages):
    smem = pl.BlockSpec(memory_space=pltpu.SMEM)
    vmem = pl.BlockSpec(memory_space=pltpu.VMEM)
    core = lax.axis_index("core").reshape(1)
    send, half = pl.pallas_call(
        pack_kernel,
        out_shape=(
            jax.ShapeDtypeStruct((PLANE, SEND_ROWS, W), jnp.bfloat16),
            jax.ShapeDtypeStruct((HALF, W), jnp.bfloat16),
        ),
        in_specs=[smem] * 4 + [vmem] * 2,
        out_specs=(pl.BlockSpec(memory_space=pl.ANY),) * 2,
        scratch_shapes=[
            pltpu.VMEM((PLANE, SEND_ROWS - ROWS, W), jnp.bfloat16),
            pltpu.SemaphoreType.DMA((PLANE + 2,)),
        ],
    )(pair_page[:, 0], pair_query, pair_label, core, queries.reshape(ROWS, W), pages[0])
    near, far = gather_column(half)
    other_near, other_far = swap_cores(near), swap_cores(far)
    got = exchange(send, ("x", "y"))
    table = got[:, ROWS, : 2 * ENTRIES].astype(jnp.int32)
    heights = (lax.axis_index("z") + jnp.array(STEPS, jnp.int32)) % NZ
    first_page = (lax.axis_index("x") * (NZ * NY) + lax.axis_index("y")).reshape(1)
    near_column = jnp.concatenate([heights[:PART], first_page])
    far_column = jnp.concatenate([heights[PART:], first_page])
    sums, far_mine, far_other = score(far_column, hot_pages, table, got, far, other_far)
    far_other = swap_cores(far_other)
    to_above = add(far_mine[2:4], far_other[2:4]).astype(jnp.bfloat16)
    to_below = add(far_mine[0:2], far_other[0:2]).astype(jnp.bfloat16)
    from_below, from_above = move(to_above, 1), move(to_below, -1)
    query_part, near_mine, near_other = score(
        near_column, hot_pages, table, got, near, other_near, sums
    )
    near_other = swap_cores(near_other)
    query_back = exchange(query_part.reshape(PLANE, ROWS, W), ("x", "y"))
    page_grad = reduce_column(near_mine, near_other, from_below, from_above)
    query_grad = jnp.sum(query_back.astype(jnp.float32), axis=0).astype(jnp.bfloat16)
    return query_grad.reshape(Q_DEV, QT, W), page_grad[None]


def solution(mesh):
    torus = Mesh(mesh.devices.reshape(NX, NZ, NY, NC), ("x", "z", "y", "core"))
    owner = ("x", "z", "y")
    device = ("x", "z", "y", "core")
    return jax.shard_map(
        shards,
        mesh=torus,
        in_specs=(P(device), P(owner), P(device), P(device), P(device), P()),
        out_specs=(P(device), P(owner, "core")),
        check_vma=False,
    )
```

```python
import functools
import math

import jax
import jax.numpy as jnp
from jax import lax
from jax.experimental import pallas as pl
from jax.experimental.pallas import tpu as pltpu
from jax.sharding import Mesh, PartitionSpec as P

SHARPNESS = 4.0
SLOPE_SCALE = 0.5
HOT_SHIFT = 2.0

NX, NZ, NY, NC = 4, 8, 4, 2
PLANE = NX * NY
QT = 32
W = 128
Q_DEV = 8
PAIR_DEV = 64
PATCHES = 1024
HALF = PATCHES // 2
CAP = 2
ROWS = Q_DEV * QT
SEND_ROWS = ROWS + 16
ENTRIES = NZ * CAP
GROUP = 8
BLOCK = 128
LOG2 = 4.0 * math.log2(math.e)
SLOTS = PLANE * CAP
LIST = SLOTS + GROUP
PART = NZ // 2
COMBINE_FLOPS = 40 * 10**9
STEPS = (0, -1, 1, 4, -2, 3, 2, -3)


def pack_kernel(
    page_ref, query_ref, label_ref, core_ref, rows_ref, whole_ref, out_ref, half_ref, table_ref, done
):
    at = pl.ds(pl.multiple_of(core_ref[0] * HALF, HALF), HALF)
    copies = [pltpu.make_async_copy(whole_ref.at[at, :], half_ref, done.at[PLANE])]
    for d in range(PLANE):
        copies.append(
            pltpu.make_async_copy(rows_ref, out_ref.at[d, pl.ds(0, ROWS), :], done.at[d])
        )
    for copy in copies:
        copy.start()
    dest = lax.broadcasted_iota(jnp.int32, (PLANE, W), 0)
    lane = lax.broadcasted_iota(jnp.int32, (PLANE, W), 1)
    entry = lane % ENTRIES
    rank = entry % CAP
    wanted = (dest // NY) * (NZ * NY) + (entry // CAP) * NY + dest % NY
    is_query = lane < ENTRIES
    is_label = jnp.logical_and(lane >= ENTRIES, lane < 2 * ENTRIES)

    def visit(i, carry):
        table, seen = carry
        hit = wanted == page_ref[i]
        value = jnp.where(is_query, query_ref[i] + 1, jnp.where(is_label, label_ref[i], 0))
        table = jnp.where(jnp.logical_and(hit, seen == rank), value, table)
        return table, seen + hit.astype(jnp.int32)

    zeros = jnp.zeros((PLANE, W), jnp.int32)
    table, _ = lax.fori_loop(0, PAIR_DEV, visit, (zeros, zeros), unroll=8)
    table = table.astype(jnp.float32)
    for d in range(PLANE):
        table_ref[d] = jnp.broadcast_to(table[d : d + 1, :], (16, W)).astype(jnp.bfloat16)
    last = pltpu.make_async_copy(
        table_ref, out_ref.at[:, pl.ds(ROWS, SEND_ROWS - ROWS), :], done.at[PLANE + 1]
    )
    last.start()
    for copy in copies:
        copy.wait()
    last.wait()


def score_kernel(
    widths, offset, column_ref, hot_ref, table_ref, got_ref, mine_ref, other_ref, carried_ref,
    query_out, mine_out, other_out,
    slot_query, slot_label, item_page, item_base, item_left, turned, query_acc, page_acc, *work,
):
    rows = GROUP * QT
    if query_acc is None:
        query_acc = query_out
    most = max(widths)
    token_refs, logit_refs, expo_refs = work[:most], work[most : 2 * most], work[2 * most :]
    if carried_ref is None:
        query_acc[...] = jnp.zeros_like(query_acc)
    else:
        query_acc[...] = carried_ref[...]
    page_acc[...] = jnp.zeros_like(page_acc)
    first_page = column_ref[PART]

    def list_page(page, items):
        height = column_ref[page]
        turned[page, :, :HALF] = mine_ref[page].T
        turned[page, :, HALF:] = other_ref[page].T
        start = page * LIST
        count = jnp.int32(0)
        for s in range(PLANE):
            for r in range(CAP):
                code = table_ref[s, height * CAP + r]
                slot_query[start + count] = s * Q_DEV + code - 1
                slot_label[start + count] = table_ref[s, ENTRIES + height * CAP + r]
                count = count + (code > 0).astype(jnp.int32)
        for g in range(GROUP - 1):
            slot_query[start + count + g] = 0
            slot_label[start + count + g] = 0
        for j in range(SLOTS // GROUP):
            item_page[items] = page
            item_base[items] = start + j * GROUP
            item_left[items] = count - j * GROUP
            items = items + (count > j * GROUP).astype(jnp.int32)
        return items

    items = lax.fori_loop(0, PART, list_page, jnp.int32(0))
    for g in range(GROUP):
        slot_query[PART * LIST + g] = 0
        slot_label[PART * LIST + g] = 0
    for u in range(most):
        item_page[items + u] = 0
        item_base[items + u] = PART * LIST
        item_left[items + u] = 0

    def per_round(width, start, step, _):
        at = [start + step * width + u for u in range(width)]
        page = [item_page[i] for i in at]
        base = [item_base[i] for i in at]
        left = [item_left[i] for i in at]
        query = [[slot_query[b + g] for g in range(GROUP)] for b in base]
        for u in range(width):
            for g in range(GROUP):
                token_refs[u][g * QT : (g + 1) * QT, :] = got_ref[
                    lax.shift_right_logical(query[u][g], 3),
                    pl.ds(pl.multiple_of(lax.bitwise_and(query[u][g], Q_DEV - 1) * QT, QT), QT),
                    :,
                ]
        dims = (((1,), (1,)), ((), ()))
        peaks, lses, inverses = [], [], []
        blocks = PATCHES // BLOCK
        tops, totals = [None] * width, [None] * width

        def multiply(u, c):
            part = (mine_ref, other_ref)[c * BLOCK // HALF]
            first = c * BLOCK % HALF
            block = lax.dot_general(
                part[page[u], first : first + BLOCK, :], token_refs[u][...], dims,
                preferred_element_type=jnp.float32,
            )
            logit_refs[u][c * BLOCK : (c + 1) * BLOCK, :] = block
            top = jnp.max(block.reshape(BLOCK // 8, 8, rows), axis=0)
            tops[u] = top if c == 0 else jnp.maximum(tops[u], top)

        def raise_e(u, c):
            piece = logit_refs[u][c * BLOCK : (c + 1) * BLOCK, :]
            e = jnp.exp2(LOG2 * (piece - peaks[u]))
            expo_refs[u][c * BLOCK : (c + 1) * BLOCK, :] = e.astype(jnp.bfloat16)
            low = jnp.sum(e.reshape(BLOCK // 8, 8, rows), axis=0)
            totals[u] = low if c == 0 else totals[u] + low

        grads = []
        for c in range(blocks):
            multiply(0, c)
        for u in range(width):
            peaks.append(jnp.max(tops[u], axis=0, keepdims=True))
            for c in range(blocks):
                if u + 1 < width:
                    multiply(u + 1, c)
                raise_e(u, c)
            total = jnp.sum(totals[u], axis=0, keepdims=True)
            lse = SHARPNESS * peaks[u] + jnp.log(total)
            lses.append(jnp.broadcast_to(lse, (W, rows)).T)
            inverses.append(jnp.broadcast_to(1.0 / total, (W, rows)).T)
            grads.append(
                jnp.dot(turned[page[u]], expo_refs[u][...], preferred_element_type=jnp.float32).T
            )
        scale = []
        for u in range(width):
            page_id = first_page + column_ref[page[u]] * NY
            hot = jnp.logical_or(hot_ref[0] == page_id, hot_ref[1] == page_id)
            shift = jnp.where(hot, HOT_SHIFT, 0.0).astype(jnp.float32)
            parts = []
            for g in range(GROUP):
                mine = slice(g * QT, (g + 1) * QT)
                score = jnp.sum(lses[u][mine], axis=0, keepdims=True) / SHARPNESS
                logit = SLOPE_SCALE * score + offset - shift
                label = slot_label[base[u] + g].astype(jnp.float32)
                live = jnp.where(g < left[u], SLOPE_SCALE, 0.0)
                slope = live * (1.0 / (1.0 + jnp.exp(-logit)) - label)
                parts.append(slope * inverses[u][mine])
            scale.append(jnp.concatenate(parts, axis=0))
        for u in range(width):
            scaled = (token_refs[u][...].astype(jnp.float32) * scale[u]).astype(jnp.bfloat16)
            page_acc[page[u]] += jnp.dot(
                expo_refs[u][...], scaled, preferred_element_type=jnp.float32
            )
        for u in range(width):
            grad = grads[u] * scale[u]
            for g in range(GROUP):
                rows_at = pl.ds(pl.multiple_of(query[u][g] * QT, QT), QT)
                query_acc[rows_at, :] += grad[g * QT : (g + 1) * QT]
        return 0

    start = jnp.int32(0)
    for width in widths:
        if width == widths[-1]:
            turns = (items - start + width - 1) // width
        else:
            turns = (items - start + 1) // width
        lax.fori_loop(0, turns, functools.partial(per_round, width, start), 0)
        start = jnp.minimum(start + turns * width, items)
    for k in range(PART):
        mine_out[k] = page_acc[k, :HALF, :].astype(jnp.bfloat16)
        other_out[k] = page_acc[k, HALF:, :].astype(jnp.bfloat16)
    if query_out is not query_acc:
        query_out[...] = query_acc[...].astype(jnp.bfloat16)


def exchange(array, axes):
    return lax.all_to_all(array, axes, split_axis=0, concat_axis=0, tiled=True)


def swap_cores(array):
    return lax.ppermute(array, "core", [(0, 1), (1, 0)])


def move(array, step):
    return lax.ppermute(array, "z", [(i, (i + step) % NZ) for i in range(NZ)])


def gather_column(half):
    below, above, across = move(half, 1), move(half, -1), move(half, 4)
    far_below = move(jnp.stack([below, across]), 1)
    far_above = move(jnp.stack([above, across]), -1)
    return jnp.stack([half, below, above, across]), jnp.concatenate([far_below, far_above])


def add(mine, other):
    return mine.astype(jnp.float32) + other.astype(jnp.float32)


def sum_kernel(parts_ref, out_ref):
    total = parts_ref[0].astype(jnp.float32)
    for s in range(1, PLANE):
        total = total + parts_ref[s].astype(jnp.float32)
    out_ref[...] = total.astype(jnp.bfloat16)


def combine_kernel(mine_ref, other_ref, below_ref, above_ref, up_ref, down_ref, over_ref):
    below, above = below_ref[...].astype(jnp.float32), above_ref[...].astype(jnp.float32)
    up_ref[...] = (add(mine_ref[2], other_ref[2]) + below[0]).astype(jnp.bfloat16)
    down_ref[...] = (add(mine_ref[1], other_ref[1]) + above[0]).astype(jnp.bfloat16)
    over_ref[...] = (add(mine_ref[3], other_ref[3]) + below[1] + above[1]).astype(jnp.bfloat16)


def reduce_column(mine, other, from_below, from_above):
    vmem = pl.BlockSpec(memory_space=pltpu.VMEM)
    up, down, over = pl.pallas_call(
        combine_kernel,
        out_shape=(jax.ShapeDtypeStruct((HALF, W), jnp.bfloat16),) * 3,
        in_specs=[vmem] * 4,
        out_specs=(vmem,) * 3,
        compiler_params=pltpu.CompilerParams(vmem_limit_bytes=6 << 20),
        cost_estimate=pl.CostEstimate(
            flops=COMBINE_FLOPS, bytes_accessed=4 << 20, transcendentals=0
        ),
    )(mine, other, from_below, from_above)
    total = add(mine[0], other[0])
    for part in (move(up, 1), move(down, -1), move(over, 4)):
        total = total + part.astype(jnp.float32)
    return total.astype(jnp.bfloat16)


def first_kernel(widths, offset, *refs):
    score_kernel(widths, offset, *refs[:6], None, *refs[6:15], None, *refs[15:])


def second_kernel(widths, offset, *refs):
    score_kernel(widths, offset, *refs)


def score(column, hot_pages, table, got, mine, other, carried=None):
    offset = -SLOPE_SCALE * QT * (math.log(PATCHES) / SHARPNESS + SHARPNESS / 2.0)
    smem = pl.BlockSpec(memory_space=pltpu.SMEM)
    vmem = pl.BlockSpec(memory_space=pltpu.VMEM)
    last = carried is not None
    widths = (4, 2)
    most = max(widths)
    pages = jax.ShapeDtypeStruct((PART, HALF, W), jnp.bfloat16)
    sums = jax.ShapeDtypeStruct((PLANE * ROWS, W), jnp.bfloat16 if last else jnp.float32)
    items = PART * SLOTS // GROUP + most
    rows = GROUP * QT
    scratch = [
        pltpu.SMEM((PART * LIST + GROUP,), jnp.int32),
        pltpu.SMEM((PART * LIST + GROUP,), jnp.int32),
        pltpu.SMEM((items,), jnp.int32),
        pltpu.SMEM((items,), jnp.int32),
        pltpu.SMEM((items,), jnp.int32),
        pltpu.VMEM((PART, W, PATCHES), jnp.bfloat16),
    ]
    scratch += [pltpu.VMEM((PLANE * ROWS, W), jnp.float32)] * last
    scratch += [pltpu.VMEM((PART, PATCHES, W), jnp.float32)]
    scratch += [pltpu.VMEM((rows, W), jnp.bfloat16)] * most
    scratch += [pltpu.VMEM((PATCHES, rows), jnp.float32)] * most
    scratch += [pltpu.VMEM((PATCHES, rows), jnp.bfloat16)] * most
    return pl.pallas_call(
        functools.partial(second_kernel if last else first_kernel, widths, offset),
        out_shape=(sums, pages, pages),
        in_specs=[smem] * 3 + [vmem] * (3 + last),
        out_specs=(vmem, vmem, vmem),
        scratch_shapes=scratch,
        compiler_params=pltpu.CompilerParams(vmem_limit_bytes=20 << 20),
        cost_estimate=pl.CostEstimate(
            flops=6 * PLANE * CAP * 2 * QT * PATCHES * W * 2,
            bytes_accessed=8 << 20,
            transcendentals=PLANE * CAP * 2 * QT * PATCHES,
        ),
    )(column, hot_pages, table, got, mine, other, *([carried] if last else []))


def shards(queries, pages, pair_page, pair_query, pair_label, hot_pages):
    smem = pl.BlockSpec(memory_space=pltpu.SMEM)
    vmem = pl.BlockSpec(memory_space=pltpu.VMEM)
    core = lax.axis_index("core").reshape(1)
    send, half = pl.pallas_call(
        pack_kernel,
        out_shape=(
            jax.ShapeDtypeStruct((PLANE, SEND_ROWS, W), jnp.bfloat16),
            jax.ShapeDtypeStruct((HALF, W), jnp.bfloat16),
        ),
        in_specs=[smem] * 4 + [vmem] * 2,
        out_specs=(pl.BlockSpec(memory_space=pl.ANY),) * 2,
        scratch_shapes=[
            pltpu.VMEM((PLANE, SEND_ROWS - ROWS, W), jnp.bfloat16),
            pltpu.SemaphoreType.DMA((PLANE + 2,)),
        ],
    )(pair_page[:, 0], pair_query, pair_label, core, queries.reshape(ROWS, W), pages[0])
    near, far = gather_column(half)
    other_near, other_far = swap_cores(near), swap_cores(far)
    got = exchange(send, ("x", "y"))
    table = got[:, ROWS, : 2 * ENTRIES].astype(jnp.int32)
    heights = (lax.axis_index("z") + jnp.array(STEPS, jnp.int32)) % NZ
    first_page = (lax.axis_index("x") * (NZ * NY) + lax.axis_index("y")).reshape(1)
    near_column = jnp.concatenate([heights[:PART], first_page])
    far_column = jnp.concatenate([heights[PART:], first_page])
    sums, far_mine, far_other = score(far_column, hot_pages, table, got, far, other_far)
    far_other = swap_cores(far_other)
    to_above = add(far_mine[2:4], far_other[2:4]).astype(jnp.bfloat16)
    to_below = add(far_mine[0:2], far_other[0:2]).astype(jnp.bfloat16)
    from_below, from_above = move(to_above, 1), move(to_below, -1)
    query_part, near_mine, near_other = score(
        near_column, hot_pages, table, got, near, other_near, sums
    )
    near_other = swap_cores(near_other)
    query_back = exchange(query_part.reshape(PLANE, ROWS, W), ("x", "y"))
    page_grad = reduce_column(near_mine, near_other, from_below, from_above)
    query_grad = pl.pallas_call(
        sum_kernel,
        out_shape=jax.ShapeDtypeStruct((ROWS, W), jnp.bfloat16),
        in_specs=[vmem],
        out_specs=vmem,
        compiler_params=pltpu.CompilerParams(vmem_limit_bytes=4 << 20),
    )(query_back)
    return query_grad.reshape(Q_DEV, QT, W), page_grad[None]


def solution(mesh):
    torus = Mesh(mesh.devices.reshape(NX, NZ, NY, NC), ("x", "z", "y", "core"))
    owner = ("x", "z", "y")
    device = ("x", "z", "y", "core")
    return jax.shard_map(
        shards,
        mesh=torus,
        in_specs=(P(device), P(owner), P(device), P(device), P(device), P()),
        out_specs=(P(device), P(owner, "core")),
        check_vma=False,
    )
```

```python
import functools
import math

import jax
import jax.numpy as jnp
from jax import lax
from jax.experimental import pallas as pl
from jax.experimental.pallas import tpu as pltpu
from jax.sharding import Mesh, PartitionSpec as P

SHARPNESS = 4.0
SLOPE_SCALE = 0.5
HOT_SHIFT = 2.0

NX, NZ, NY, NC = 4, 8, 4, 2
PLANE = NX * NY
QT = 32
W = 128
Q_DEV = 8
PAIR_DEV = 64
PATCHES = 1024
HALF = PATCHES // 2
CAP = 2
ROWS = Q_DEV * QT
SEND_ROWS = ROWS + 16
ENTRIES = NZ * CAP
GROUP = 8
BLOCK = 128
LOG2 = 4.0 * math.log2(math.e)
SLOTS = PLANE * CAP
LIST = SLOTS + GROUP
PART = NZ // 2
COMBINE_FLOPS = 40 * 10**9
STEPS = (0, -1, 1, 4, -2, 3, 2, -3)


def pack_kernel(
    page_ref, query_ref, label_ref, core_ref, rows_ref, whole_ref, out_ref, half_ref, table_ref, done
):
    at = pl.ds(pl.multiple_of(core_ref[0] * HALF, HALF), HALF)
    copies = [pltpu.make_async_copy(whole_ref.at[at, :], half_ref, done.at[PLANE])]
    for d in range(PLANE):
        copies.append(
            pltpu.make_async_copy(rows_ref, out_ref.at[d, pl.ds(0, ROWS), :], done.at[d])
        )
    for copy in copies:
        copy.start()
    dest = lax.broadcasted_iota(jnp.int32, (PLANE, W), 0)
    lane = lax.broadcasted_iota(jnp.int32, (PLANE, W), 1)
    entry = lane % ENTRIES
    rank = entry % CAP
    wanted = (dest // NY) * (NZ * NY) + (entry // CAP) * NY + dest % NY
    is_query = lane < ENTRIES
    is_label = jnp.logical_and(lane >= ENTRIES, lane < 2 * ENTRIES)

    def visit(i, carry):
        table, seen = carry
        hit = wanted == page_ref[i]
        value = jnp.where(is_query, query_ref[i] + 1, jnp.where(is_label, label_ref[i], 0))
        table = jnp.where(jnp.logical_and(hit, seen == rank), value, table)
        return table, seen + hit.astype(jnp.int32)

    zeros = jnp.zeros((PLANE, W), jnp.int32)
    table, _ = lax.fori_loop(0, PAIR_DEV, visit, (zeros, zeros), unroll=8)
    table = table.astype(jnp.float32)
    for d in range(PLANE):
        table_ref[d] = jnp.broadcast_to(table[d : d + 1, :], (16, W)).astype(jnp.bfloat16)
    last = pltpu.make_async_copy(
        table_ref, out_ref.at[:, pl.ds(ROWS, SEND_ROWS - ROWS), :], done.at[PLANE + 1]
    )
    last.start()
    for copy in copies:
        copy.wait()
    last.wait()


def score_kernel(
    widths, offset, column_ref, hot_ref, table_ref, got_ref, mine_ref, other_ref, carried_ref,
    query_out, mine_out, other_out,
    slot_query, slot_label, item_page, item_base, item_left, turned, query_acc, page_acc, *work,
):
    rows = GROUP * QT
    if query_acc is None:
        query_acc = query_out
    most = max(widths)
    token_refs, logit_refs, expo_refs = work[:most], work[most : 2 * most], work[2 * most :]
    if carried_ref is None:
        query_acc[...] = jnp.zeros_like(query_acc)
    else:
        query_acc[...] = carried_ref[...]
    page_acc[...] = jnp.zeros_like(page_acc)
    first_page = column_ref[PART]

    def list_page(page, items):
        height = column_ref[page]
        turned[page, :, :HALF] = mine_ref[page].T
        turned[page, :, HALF:] = other_ref[page].T
        start = page * LIST
        count = jnp.int32(0)
        for s in range(PLANE):
            for r in range(CAP):
                code = table_ref[s, height * CAP + r]
                slot_query[start + count] = s * Q_DEV + code - 1
                slot_label[start + count] = table_ref[s, ENTRIES + height * CAP + r]
                count = count + (code > 0).astype(jnp.int32)
        for g in range(GROUP - 1):
            slot_query[start + count + g] = 0
            slot_label[start + count + g] = 0
        for j in range(SLOTS // GROUP):
            item_page[items] = page
            item_base[items] = start + j * GROUP
            item_left[items] = count - j * GROUP
            items = items + (count > j * GROUP).astype(jnp.int32)
        return items

    items = lax.fori_loop(0, PART, list_page, jnp.int32(0))
    for g in range(GROUP):
        slot_query[PART * LIST + g] = 0
        slot_label[PART * LIST + g] = 0
    for u in range(most):
        item_page[items + u] = 0
        item_base[items + u] = PART * LIST
        item_left[items + u] = 0

    def per_round(width, start, step, _):
        at = [start + step * width + u for u in range(width)]
        page = [item_page[i] for i in at]
        base = [item_base[i] for i in at]
        left = [item_left[i] for i in at]
        query = [[slot_query[b + g] for g in range(GROUP)] for b in base]
        for u in range(width):
            for g in range(GROUP):
                token_refs[u][g * QT : (g + 1) * QT, :] = got_ref[
                    lax.shift_right_logical(query[u][g], 3),
                    pl.ds(pl.multiple_of(lax.bitwise_and(query[u][g], Q_DEV - 1) * QT, QT), QT),
                    :,
                ]
        dims = (((1,), (1,)), ((), ()))
        peaks, lses, inverses = [], [], []
        blocks = PATCHES // BLOCK
        tops, totals = [None] * width, [None] * width

        def multiply(u, c):
            part = (mine_ref, other_ref)[c * BLOCK // HALF]
            first = c * BLOCK % HALF
            block = lax.dot_general(
                part[page[u], first : first + BLOCK, :], token_refs[u][...], dims,
                preferred_element_type=jnp.float32,
            )
            logit_refs[u][c * BLOCK : (c + 1) * BLOCK, :] = block
            top = jnp.max(block.reshape(BLOCK // 8, 8, rows), axis=0)
            tops[u] = top if c == 0 else jnp.maximum(tops[u], top)

        def raise_e(u, c):
            piece = logit_refs[u][c * BLOCK : (c + 1) * BLOCK, :]
            e = jnp.exp2(LOG2 * (piece - peaks[u]))
            expo_refs[u][c * BLOCK : (c + 1) * BLOCK, :] = e.astype(jnp.bfloat16)
            low = jnp.sum(e.reshape(BLOCK // 8, 8, rows), axis=0)
            totals[u] = low if c == 0 else totals[u] + low

        grads = []
        for c in range(blocks):
            multiply(0, c)
        for u in range(width):
            peaks.append(jnp.max(tops[u], axis=0, keepdims=True))
            for c in range(blocks):
                if u + 1 < width:
                    multiply(u + 1, c)
                raise_e(u, c)
            total = jnp.sum(totals[u], axis=0, keepdims=True)
            lse = SHARPNESS * peaks[u] + jnp.log(total)
            lses.append(jnp.broadcast_to(lse, (W, rows)).T)
            inverses.append(jnp.broadcast_to(1.0 / total, (W, rows)).T)
            grads.append(
                jnp.dot(turned[page[u]], expo_refs[u][...], preferred_element_type=jnp.float32).T
            )
        scale = []
        for u in range(width):
            page_id = first_page + column_ref[page[u]] * NY
            hot = jnp.logical_or(hot_ref[0] == page_id, hot_ref[1] == page_id)
            shift = jnp.where(hot, HOT_SHIFT, 0.0).astype(jnp.float32)
            parts = []
            for g in range(GROUP):
                mine = slice(g * QT, (g + 1) * QT)
                score = jnp.sum(lses[u][mine], axis=0, keepdims=True) / SHARPNESS
                logit = SLOPE_SCALE * score + offset - shift
                label = slot_label[base[u] + g].astype(jnp.float32)
                live = jnp.where(g < left[u], SLOPE_SCALE, 0.0)
                slope = live * (1.0 / (1.0 + jnp.exp(-logit)) - label)
                parts.append(slope * inverses[u][mine])
            scale.append(jnp.concatenate(parts, axis=0))
        for u in range(width):
            scaled = (token_refs[u][...].astype(jnp.float32) * scale[u]).astype(jnp.bfloat16)
            page_acc[page[u]] += jnp.dot(
                expo_refs[u][...], scaled, preferred_element_type=jnp.float32
            )
        for u in range(width):
            grad = grads[u] * scale[u]
            for g in range(GROUP):
                rows_at = pl.ds(pl.multiple_of(query[u][g] * QT, QT), QT)
                query_acc[rows_at, :] += grad[g * QT : (g + 1) * QT]
        return 0

    start = jnp.int32(0)
    for width in widths:
        if width == widths[-1]:
            turns = (items - start + width - 1) // width
        else:
            turns = (items - start + 1) // width
        lax.fori_loop(0, turns, functools.partial(per_round, width, start), 0)
        start = jnp.minimum(start + turns * width, items)
    for k in range(PART):
        mine_out[k] = page_acc[k, :HALF, :].astype(jnp.bfloat16)
        other_out[k] = page_acc[k, HALF:, :].astype(jnp.bfloat16)
    if query_out is not query_acc:
        query_out[...] = query_acc[...].astype(jnp.bfloat16)


def exchange(array, axes):
    return lax.all_to_all(array, axes, split_axis=0, concat_axis=0, tiled=True)


def swap_cores(array):
    return lax.ppermute(array, "core", [(0, 1), (1, 0)])


def move(array, step):
    return lax.ppermute(array, "z", [(i, (i + step) % NZ) for i in range(NZ)])


def gather_column(half):
    across, below, above = move(half, 4), move(half, 1), move(half, -1)
    far_below = move(jnp.stack([below, across]), 1)
    far_above = move(jnp.stack([above, across]), -1)
    return jnp.stack([half, below, above, across]), jnp.concatenate([far_below, far_above])


def add(mine, other):
    return mine.astype(jnp.float32) + other.astype(jnp.float32)


def sum_kernel(parts_ref, out_ref):
    total = parts_ref[0].astype(jnp.float32)
    for s in range(1, PLANE):
        total = total + parts_ref[s].astype(jnp.float32)
    out_ref[...] = total.astype(jnp.bfloat16)


def combine_kernel(mine_ref, other_ref, below_ref, above_ref, up_ref, down_ref, over_ref):
    below, above = below_ref[...].astype(jnp.float32), above_ref[...].astype(jnp.float32)
    up_ref[...] = (add(mine_ref[2], other_ref[2]) + below[0]).astype(jnp.bfloat16)
    down_ref[...] = (add(mine_ref[1], other_ref[1]) + above[0]).astype(jnp.bfloat16)
    over_ref[...] = (add(mine_ref[3], other_ref[3]) + below[1] + above[1]).astype(jnp.bfloat16)


def reduce_column(mine, other, from_below, from_above):
    vmem = pl.BlockSpec(memory_space=pltpu.VMEM)
    up, down, over = pl.pallas_call(
        combine_kernel,
        out_shape=(jax.ShapeDtypeStruct((HALF, W), jnp.bfloat16),) * 3,
        in_specs=[vmem] * 4,
        out_specs=(vmem,) * 3,
        compiler_params=pltpu.CompilerParams(vmem_limit_bytes=6 << 20),
        cost_estimate=pl.CostEstimate(
            flops=COMBINE_FLOPS, bytes_accessed=4 << 20, transcendentals=0
        ),
    )(mine, other, from_below, from_above)
    total = add(mine[0], other[0])
    for part in (move(over, 4), move(up, 1), move(down, -1)):
        total = total + part.astype(jnp.float32)
    return total.astype(jnp.bfloat16)


def first_kernel(widths, offset, *refs):
    score_kernel(widths, offset, *refs[:6], None, *refs[6:15], None, *refs[15:])


def second_kernel(widths, offset, *refs):
    score_kernel(widths, offset, *refs)


def score(column, hot_pages, table, got, mine, other, carried=None):
    offset = -SLOPE_SCALE * QT * (math.log(PATCHES) / SHARPNESS + SHARPNESS / 2.0)
    smem = pl.BlockSpec(memory_space=pltpu.SMEM)
    vmem = pl.BlockSpec(memory_space=pltpu.VMEM)
    last = carried is not None
    widths = (4, 2)
    most = max(widths)
    pages = jax.ShapeDtypeStruct((PART, HALF, W), jnp.bfloat16)
    sums = jax.ShapeDtypeStruct((PLANE * ROWS, W), jnp.bfloat16 if last else jnp.float32)
    items = PART * SLOTS // GROUP + most
    rows = GROUP * QT
    scratch = [
        pltpu.SMEM((PART * LIST + GROUP,), jnp.int32),
        pltpu.SMEM((PART * LIST + GROUP,), jnp.int32),
        pltpu.SMEM((items,), jnp.int32),
        pltpu.SMEM((items,), jnp.int32),
        pltpu.SMEM((items,), jnp.int32),
        pltpu.VMEM((PART, W, PATCHES), jnp.bfloat16),
    ]
    scratch += [pltpu.VMEM((PLANE * ROWS, W), jnp.float32)] * last
    scratch += [pltpu.VMEM((PART, PATCHES, W), jnp.float32)]
    scratch += [pltpu.VMEM((rows, W), jnp.bfloat16)] * most
    scratch += [pltpu.VMEM((PATCHES, rows), jnp.float32)] * most
    scratch += [pltpu.VMEM((PATCHES, rows), jnp.bfloat16)] * most
    return pl.pallas_call(
        functools.partial(second_kernel if last else first_kernel, widths, offset),
        out_shape=(sums, pages, pages),
        in_specs=[smem] * 3 + [vmem] * (3 + last),
        out_specs=(vmem, vmem, vmem),
        scratch_shapes=scratch,
        compiler_params=pltpu.CompilerParams(vmem_limit_bytes=20 << 20),
        cost_estimate=pl.CostEstimate(
            flops=6 * PLANE * CAP * 2 * QT * PATCHES * W * 2,
            bytes_accessed=8 << 20,
            transcendentals=PLANE * CAP * 2 * QT * PATCHES,
        ),
    )(column, hot_pages, table, got, mine, other, *([carried] if last else []))


def shards(queries, pages, pair_page, pair_query, pair_label, hot_pages):
    smem = pl.BlockSpec(memory_space=pltpu.SMEM)
    vmem = pl.BlockSpec(memory_space=pltpu.VMEM)
    core = lax.axis_index("core").reshape(1)
    send, half = pl.pallas_call(
        pack_kernel,
        out_shape=(
            jax.ShapeDtypeStruct((PLANE, SEND_ROWS, W), jnp.bfloat16),
            jax.ShapeDtypeStruct((HALF, W), jnp.bfloat16),
        ),
        in_specs=[smem] * 4 + [vmem] * 2,
        out_specs=(pl.BlockSpec(memory_space=pl.ANY),) * 2,
        scratch_shapes=[
            pltpu.VMEM((PLANE, SEND_ROWS - ROWS, W), jnp.bfloat16),
            pltpu.SemaphoreType.DMA((PLANE + 2,)),
        ],
    )(pair_page[:, 0], pair_query, pair_label, core, queries.reshape(ROWS, W), pages[0])
    near, far = gather_column(half)
    other_near, other_far = swap_cores(near), swap_cores(far)
    got = exchange(send, ("x", "y"))
    table = got[:, ROWS, : 2 * ENTRIES].astype(jnp.int32)
    heights = (lax.axis_index("z") + jnp.array(STEPS, jnp.int32)) % NZ
    first_page = (lax.axis_index("x") * (NZ * NY) + lax.axis_index("y")).reshape(1)
    near_column = jnp.concatenate([heights[:PART], first_page])
    far_column = jnp.concatenate([heights[PART:], first_page])
    sums, far_mine, far_other = score(far_column, hot_pages, table, got, far, other_far)
    far_other = swap_cores(far_other)
    to_above = add(far_mine[2:4], far_other[2:4]).astype(jnp.bfloat16)
    to_below = add(far_mine[0:2], far_other[0:2]).astype(jnp.bfloat16)
    from_below, from_above = move(to_above, 1), move(to_below, -1)
    query_part, near_mine, near_other = score(
        near_column, hot_pages, table, got, near, other_near, sums
    )
    near_other = swap_cores(near_other)
    query_back = exchange(query_part.reshape(PLANE, ROWS, W), ("x", "y"))
    page_grad = reduce_column(near_mine, near_other, from_below, from_above)
    query_grad = pl.pallas_call(
        sum_kernel,
        out_shape=jax.ShapeDtypeStruct((ROWS, W), jnp.bfloat16),
        in_specs=[vmem],
        out_specs=vmem,
        compiler_params=pltpu.CompilerParams(vmem_limit_bytes=4 << 20),
    )(query_back)
    return query_grad.reshape(Q_DEV, QT, W), page_grad[None]


def solution(mesh):
    torus = Mesh(mesh.devices.reshape(NX, NZ, NY, NC), ("x", "z", "y", "core"))
    owner = ("x", "z", "y")
    device = ("x", "z", "y", "core")
    return jax.shard_map(
        shards,
        mesh=torus,
        in_specs=(P(device), P(owner), P(device), P(device), P(device), P()),
        out_specs=(P(device), P(owner, "core")),
        check_vma=False,
    )
```

```python
import functools
import math

import jax
import jax.numpy as jnp
from jax import lax
from jax.experimental import pallas as pl
from jax.experimental.pallas import tpu as pltpu
from jax.sharding import Mesh, PartitionSpec as P

SHARPNESS = 4.0
SLOPE_SCALE = 0.5
HOT_SHIFT = 2.0

NX, NZ, NY, NC = 4, 8, 4, 2
PLANE = NX * NY
QT = 32
W = 128
Q_DEV = 8
PAIR_DEV = 64
PATCHES = 1024
HALF = PATCHES // 2
CAP = 2
ROWS = Q_DEV * QT
SEND_ROWS = ROWS + 16
ENTRIES = NZ * CAP
GROUP = 8
BLOCK = 128
LOG2 = 4.0 * math.log2(math.e)
SLOTS = PLANE * CAP
LIST = SLOTS + GROUP
PART = NZ // 2
COMBINE_FLOPS = 40 * 10**9
STEPS = (0, -1, 1, 4, -2, 3, 2, -3)


def pack_kernel(
    page_ref, query_ref, label_ref, core_ref, rows_ref, whole_ref, out_ref, half_ref, table_ref, done
):
    at = pl.ds(pl.multiple_of(core_ref[0] * HALF, HALF), HALF)
    copies = [pltpu.make_async_copy(whole_ref.at[at, :], half_ref, done.at[PLANE])]
    for d in range(PLANE):
        copies.append(
            pltpu.make_async_copy(rows_ref, out_ref.at[d, pl.ds(0, ROWS), :], done.at[d])
        )
    for copy in copies:
        copy.start()
    dest = lax.broadcasted_iota(jnp.int32, (PLANE, W), 0)
    lane = lax.broadcasted_iota(jnp.int32, (PLANE, W), 1)
    entry = lane % ENTRIES
    rank = entry % CAP
    wanted = (dest // NY) * (NZ * NY) + (entry // CAP) * NY + dest % NY
    is_query = lane < ENTRIES
    is_label = jnp.logical_and(lane >= ENTRIES, lane < 2 * ENTRIES)

    def visit(i, carry):
        table, seen = carry
        hit = wanted == page_ref[i]
        value = jnp.where(is_query, query_ref[i] + 1, jnp.where(is_label, label_ref[i], 0))
        table = jnp.where(jnp.logical_and(hit, seen == rank), value, table)
        return table, seen + hit.astype(jnp.int32)

    zeros = jnp.zeros((PLANE, W), jnp.int32)
    table, _ = lax.fori_loop(0, PAIR_DEV, visit, (zeros, zeros), unroll=8)
    table = table.astype(jnp.float32)
    for d in range(PLANE):
        table_ref[d] = jnp.broadcast_to(table[d : d + 1, :], (16, W)).astype(jnp.bfloat16)
    last = pltpu.make_async_copy(
        table_ref, out_ref.at[:, pl.ds(ROWS, SEND_ROWS - ROWS), :], done.at[PLANE + 1]
    )
    last.start()
    for copy in copies:
        copy.wait()
    last.wait()


def score_kernel(
    widths, offset, column_ref, hot_ref, table_ref, got_ref, mine_ref, other_ref, carried_ref,
    query_out, mine_out, other_out,
    slot_query, slot_label, item_page, item_base, item_left, turned, query_acc, page_acc, *work,
):
    rows = GROUP * QT
    if query_acc is None:
        query_acc = query_out
    most = max(widths)
    token_refs, logit_refs, expo_refs = work[:most], work[most : 2 * most], work[2 * most :]
    if carried_ref is None:
        query_acc[...] = jnp.zeros_like(query_acc)
    else:
        query_acc[...] = carried_ref[...]
    page_acc[...] = jnp.zeros_like(page_acc)
    first_page = column_ref[PART]

    def list_page(page, items):
        height = column_ref[page]
        turned[page, :, :HALF] = mine_ref[page].T
        turned[page, :, HALF:] = other_ref[page].T
        start = page * LIST
        count = jnp.int32(0)
        for s in range(PLANE):
            for r in range(CAP):
                code = table_ref[s, height * CAP + r]
                slot_query[start + count] = s * Q_DEV + code - 1
                slot_label[start + count] = table_ref[s, ENTRIES + height * CAP + r]
                count = count + (code > 0).astype(jnp.int32)
        for g in range(GROUP - 1):
            slot_query[start + count + g] = 0
            slot_label[start + count + g] = 0
        for j in range(SLOTS // GROUP):
            item_page[items] = page
            item_base[items] = start + j * GROUP
            item_left[items] = count - j * GROUP
            items = items + (count > j * GROUP).astype(jnp.int32)
        return items

    items = lax.fori_loop(0, PART, list_page, jnp.int32(0))
    for g in range(GROUP):
        slot_query[PART * LIST + g] = 0
        slot_label[PART * LIST + g] = 0
    for u in range(most):
        item_page[items + u] = 0
        item_base[items + u] = PART * LIST
        item_left[items + u] = 0

    def per_round(width, start, step, _):
        at = [start + step * width + u for u in range(width)]
        page = [item_page[i] for i in at]
        base = [item_base[i] for i in at]
        left = [item_left[i] for i in at]
        query = [[slot_query[b + g] for g in range(GROUP)] for b in base]
        for u in range(width):
            for g in range(GROUP):
                token_refs[u][g * QT : (g + 1) * QT, :] = got_ref[
                    lax.shift_right_logical(query[u][g], 3),
                    pl.ds(pl.multiple_of(lax.bitwise_and(query[u][g], Q_DEV - 1) * QT, QT), QT),
                    :,
                ]
        dims = (((1,), (1,)), ((), ()))
        peaks, lses, inverses = [], [], []
        blocks = PATCHES // BLOCK
        tops, totals = [None] * width, [None] * width

        def multiply(u, c):
            part = (mine_ref, other_ref)[c * BLOCK // HALF]
            first = c * BLOCK % HALF
            block = lax.dot_general(
                part[page[u], first : first + BLOCK, :], token_refs[u][...], dims,
                preferred_element_type=jnp.float32,
            )
            logit_refs[u][c * BLOCK : (c + 1) * BLOCK, :] = block
            top = jnp.max(block.reshape(BLOCK // 8, 8, rows), axis=0)
            tops[u] = top if c == 0 else jnp.maximum(tops[u], top)

        def raise_e(u, c):
            piece = logit_refs[u][c * BLOCK : (c + 1) * BLOCK, :]
            e = jnp.exp2(LOG2 * (piece - peaks[u]))
            expo_refs[u][c * BLOCK : (c + 1) * BLOCK, :] = e.astype(jnp.bfloat16)
            low = jnp.sum(e.reshape(BLOCK // 8, 8, rows), axis=0)
            totals[u] = low if c == 0 else totals[u] + low

        grads = []
        for c in range(blocks):
            multiply(0, c)
        for u in range(width):
            peaks.append(jnp.max(tops[u], axis=0, keepdims=True))
            for c in range(blocks):
                if u + 1 < width:
                    multiply(u + 1, c)
                raise_e(u, c)
            total = jnp.sum(totals[u], axis=0, keepdims=True)
            lse = SHARPNESS * peaks[u] + jnp.log(total)
            lses.append(jnp.broadcast_to(lse, (W, rows)).T)
            inverses.append(jnp.broadcast_to(1.0 / total, (W, rows)).T)
            grads.append(
                jnp.dot(turned[page[u]], expo_refs[u][...], preferred_element_type=jnp.float32).T
            )
        scale = []
        for u in range(width):
            page_id = first_page + column_ref[page[u]] * NY
            hot = jnp.logical_or(hot_ref[0] == page_id, hot_ref[1] == page_id)
            shift = jnp.where(hot, HOT_SHIFT, 0.0).astype(jnp.float32)
            parts = []
            for g in range(GROUP):
                mine = slice(g * QT, (g + 1) * QT)
                score = jnp.sum(lses[u][mine], axis=0, keepdims=True) / SHARPNESS
                logit = SLOPE_SCALE * score + offset - shift
                label = slot_label[base[u] + g].astype(jnp.float32)
                live = jnp.where(g < left[u], SLOPE_SCALE, 0.0)
                slope = live * (1.0 / (1.0 + jnp.exp(-logit)) - label)
                parts.append(slope * inverses[u][mine])
            scale.append(jnp.concatenate(parts, axis=0))
        for u in range(width):
            scaled = (token_refs[u][...].astype(jnp.float32) * scale[u]).astype(jnp.bfloat16)
            page_acc[page[u]] += jnp.dot(
                expo_refs[u][...], scaled, preferred_element_type=jnp.float32
            )
        for u in range(width):
            grad = grads[u] * scale[u]
            for g in range(GROUP):
                rows_at = pl.ds(pl.multiple_of(query[u][g] * QT, QT), QT)
                query_acc[rows_at, :] += grad[g * QT : (g + 1) * QT]
        return 0

    start = jnp.int32(0)
    for width in widths:
        if width == widths[-1]:
            turns = (items - start + width - 1) // width
        else:
            turns = (items - start + 1) // width
        lax.fori_loop(0, turns, functools.partial(per_round, width, start), 0)
        start = jnp.minimum(start + turns * width, items)
    for k in range(PART):
        mine_out[k] = page_acc[k, :HALF, :].astype(jnp.bfloat16)
        other_out[k] = page_acc[k, HALF:, :].astype(jnp.bfloat16)
    if query_out is not query_acc:
        query_out[...] = query_acc[...].astype(jnp.bfloat16)


def exchange(array, axes):
    return lax.all_to_all(array, axes, split_axis=0, concat_axis=0, tiled=True)


def swap_cores(array):
    return lax.ppermute(array, "core", [(0, 1), (1, 0)])


def move(array, step):
    return lax.ppermute(array, "z", [(i, (i + step) % NZ) for i in range(NZ)])


def gather_column(half):
    across, below, above = move(half, 4), move(half, 1), move(half, -1)
    far_below = move(jnp.stack([below, across]), 1)
    far_above = move(jnp.stack([above, across]), -1)
    return jnp.stack([half, below, above, across]), jnp.concatenate([far_below, far_above])


def add(mine, other):
    return mine.astype(jnp.float32) + other.astype(jnp.float32)


def sum_kernel(parts_ref, out_ref):
    total = parts_ref[0].astype(jnp.float32)
    for s in range(1, PLANE):
        total = total + parts_ref[s].astype(jnp.float32)
    out_ref[...] = total.astype(jnp.bfloat16)


def far_kernel(mine_ref, other_ref, below_ref, above_ref):
    far = PART // 2
    below_ref[...] = add(mine_ref[:far], other_ref[:far]).astype(jnp.bfloat16)
    above_ref[...] = add(mine_ref[far:], other_ref[far:]).astype(jnp.bfloat16)


def combine_kernel(mine_ref, other_ref, below_ref, above_ref, up_ref, down_ref, over_ref):
    below, above = below_ref[...].astype(jnp.float32), above_ref[...].astype(jnp.float32)
    up_ref[...] = (add(mine_ref[2], other_ref[2]) + below[0]).astype(jnp.bfloat16)
    down_ref[...] = (add(mine_ref[1], other_ref[1]) + above[0]).astype(jnp.bfloat16)
    over_ref[...] = (add(mine_ref[3], other_ref[3]) + below[1] + above[1]).astype(jnp.bfloat16)


def reduce_column(mine, other, from_below, from_above):
    vmem = pl.BlockSpec(memory_space=pltpu.VMEM)
    up, down, over = pl.pallas_call(
        combine_kernel,
        out_shape=(jax.ShapeDtypeStruct((HALF, W), jnp.bfloat16),) * 3,
        in_specs=[vmem] * 4,
        out_specs=(vmem,) * 3,
        compiler_params=pltpu.CompilerParams(vmem_limit_bytes=6 << 20),
        cost_estimate=pl.CostEstimate(
            flops=COMBINE_FLOPS, bytes_accessed=4 << 20, transcendentals=0
        ),
    )(mine, other, from_below, from_above)
    total = add(mine[0], other[0])
    for part in (move(over, 4), move(up, 1), move(down, -1)):
        total = total + part.astype(jnp.float32)
    return total.astype(jnp.bfloat16)


def first_kernel(widths, offset, *refs):
    score_kernel(widths, offset, *refs[:6], None, *refs[6:15], None, *refs[15:])


def second_kernel(widths, offset, *refs):
    score_kernel(widths, offset, *refs)


def score(column, hot_pages, table, got, mine, other, carried=None):
    offset = -SLOPE_SCALE * QT * (math.log(PATCHES) / SHARPNESS + SHARPNESS / 2.0)
    smem = pl.BlockSpec(memory_space=pltpu.SMEM)
    vmem = pl.BlockSpec(memory_space=pltpu.VMEM)
    last = carried is not None
    widths = (4, 2)
    most = max(widths)
    pages = jax.ShapeDtypeStruct((PART, HALF, W), jnp.bfloat16)
    sums = jax.ShapeDtypeStruct((PLANE * ROWS, W), jnp.bfloat16 if last else jnp.float32)
    items = PART * SLOTS // GROUP + most
    rows = GROUP * QT
    scratch = [
        pltpu.SMEM((PART * LIST + GROUP,), jnp.int32),
        pltpu.SMEM((PART * LIST + GROUP,), jnp.int32),
        pltpu.SMEM((items,), jnp.int32),
        pltpu.SMEM((items,), jnp.int32),
        pltpu.SMEM((items,), jnp.int32),
        pltpu.VMEM((PART, W, PATCHES), jnp.bfloat16),
    ]
    scratch += [pltpu.VMEM((PLANE * ROWS, W), jnp.float32)] * last
    scratch += [pltpu.VMEM((PART, PATCHES, W), jnp.float32)]
    scratch += [pltpu.VMEM((rows, W), jnp.bfloat16)] * most
    scratch += [pltpu.VMEM((PATCHES, rows), jnp.float32)] * most
    scratch += [pltpu.VMEM((PATCHES, rows), jnp.bfloat16)] * most
    return pl.pallas_call(
        functools.partial(second_kernel if last else first_kernel, widths, offset),
        out_shape=(sums, pages, pages),
        in_specs=[smem] * 3 + [vmem] * (3 + last),
        out_specs=(vmem, vmem, vmem),
        scratch_shapes=scratch,
        compiler_params=pltpu.CompilerParams(vmem_limit_bytes=20 << 20),
        cost_estimate=pl.CostEstimate(
            flops=6 * PLANE * CAP * 2 * QT * PATCHES * W * 2,
            bytes_accessed=8 << 20,
            transcendentals=PLANE * CAP * 2 * QT * PATCHES,
        ),
    )(column, hot_pages, table, got, mine, other, *([carried] if last else []))


def shards(queries, pages, pair_page, pair_query, pair_label, hot_pages):
    smem = pl.BlockSpec(memory_space=pltpu.SMEM)
    vmem = pl.BlockSpec(memory_space=pltpu.VMEM)
    core = lax.axis_index("core").reshape(1)
    send, half = pl.pallas_call(
        pack_kernel,
        out_shape=(
            jax.ShapeDtypeStruct((PLANE, SEND_ROWS, W), jnp.bfloat16),
            jax.ShapeDtypeStruct((HALF, W), jnp.bfloat16),
        ),
        in_specs=[smem] * 4 + [vmem] * 2,
        out_specs=(pl.BlockSpec(memory_space=pl.ANY),) * 2,
        scratch_shapes=[
            pltpu.VMEM((PLANE, SEND_ROWS - ROWS, W), jnp.bfloat16),
            pltpu.SemaphoreType.DMA((PLANE + 2,)),
        ],
    )(pair_page[:, 0], pair_query, pair_label, core, queries.reshape(ROWS, W), pages[0])
    near, far = gather_column(half)
    other_near, other_far = swap_cores(near), swap_cores(far)
    got = exchange(send, ("x", "y"))
    table = got[:, ROWS, : 2 * ENTRIES].astype(jnp.int32)
    heights = (lax.axis_index("z") + jnp.array(STEPS, jnp.int32)) % NZ
    first_page = (lax.axis_index("x") * (NZ * NY) + lax.axis_index("y")).reshape(1)
    near_column = jnp.concatenate([heights[:PART], first_page])
    far_column = jnp.concatenate([heights[PART:], first_page])
    sums, far_mine, far_other = score(far_column, hot_pages, table, got, far, other_far)
    far_other = swap_cores(far_other)
    to_below, to_above = pl.pallas_call(
        far_kernel,
        out_shape=(jax.ShapeDtypeStruct((PART // 2, HALF, W), jnp.bfloat16),) * 2,
        in_specs=[vmem] * 2,
        out_specs=(vmem,) * 2,
        compiler_params=pltpu.CompilerParams(vmem_limit_bytes=4 << 20),
    )(far_mine, far_other)
    from_below, from_above = move(to_above, 1), move(to_below, -1)
    query_part, near_mine, near_other = score(
        near_column, hot_pages, table, got, near, other_near, sums
    )
    near_other = swap_cores(near_other)
    query_back = exchange(query_part.reshape(PLANE, ROWS, W), ("x", "y"))
    page_grad = reduce_column(near_mine, near_other, from_below, from_above)
    query_grad = pl.pallas_call(
        sum_kernel,
        out_shape=jax.ShapeDtypeStruct((ROWS, W), jnp.bfloat16),
        in_specs=[vmem],
        out_specs=vmem,
        compiler_params=pltpu.CompilerParams(vmem_limit_bytes=4 << 20),
    )(query_back)
    return query_grad.reshape(Q_DEV, QT, W), page_grad[None]


def solution(mesh):
    torus = Mesh(mesh.devices.reshape(NX, NZ, NY, NC), ("x", "z", "y", "core"))
    owner = ("x", "z", "y")
    device = ("x", "z", "y", "core")
    return jax.shard_map(
        shards,
        mesh=torus,
        in_specs=(P(device), P(owner), P(device), P(device), P(device), P()),
        out_specs=(P(device), P(owner, "core")),
        check_vma=False,
    )
```
